128 devices in a mesh: space: 8 (over y, core), chan: 16 (over z, x).
Axes of the slice: x: 4, y: 4, z: 4, core: 2. Of those that a mesh axis runs over, the one named last changes fastest.
Arguments:
- volume: bfloat16 [4, 64, 64, 64, 128], P(None, 'space', 'chan'), may hold values from -6 to 6
- w_first: bfloat16 [3, 3, 3, 128, 256], P(None, None, None, None, 'chan'), may hold values from -0.109375 to 0.109375
- w_second: bfloat16 [3, 3, 3, 256, 256], P(None, None, None, None, 'chan'), may hold values from -0.078125 to 0.078125
- cotangent: bfloat16 [4, 16, 16, 16, 256], P(None, 'space', None, None, 'chan'), may hold values from -6 to 6
Outputs:
- second_out: bfloat16 [4, 16, 16, 16, 256], P(None, 'space', None, None, 'chan')
- volume_grad: bfloat16 [4, 64, 64, 64, 128], P(None, 'space', 'chan')
- first_grad: float32 [3, 3, 3, 128, 256], P(None, None, None, None, 'chan')
- second_grad: float32 [3, 3, 3, 256, 256], P(None, None, None, None, 'chan')
The draws below stay inside these ranges and needn't reach their ends.
All inputs are finite; a program needn't handle non-finite values.
Results may differ from the reference program's by a relative error of at most 0.018.
Values may be sent and summed in bfloat16 or wider, within the bound.
A program may use at most 64 MiB of HBM per device.

```python
import jax
import jax.numpy as jnp

VOLS = 4
DEPTH = 64
C_IN = 128
C_MID = 256
C_OUT = 256
SIDE_X = 64
SIDE_Y = 64


def levels(own_key, shape, pieces, least, largest):
    def one(dim, blocks):
        heights = jax.random.uniform(jax.random.fold_in(jax.random.fold_in(own_key, 6), dim), (blocks,), jnp.float32, least / len(pieces), largest / len(pieces))
        return jnp.repeat(jnp.exp(heights), shape[dim] // blocks).reshape((-1,) + (1,) * (len(shape) - dim - 1))

    loudness = one(*pieces[0])
    for cut in pieces[1:]:
        loudness = loudness * one(*cut)
    return loudness


def gaussian(key, shape, deviation, reach, shards=(), kind=jnp.bfloat16):
    level = levels(key, shape, shards, -0.22, 0.18) if shards else 1.0
    values = jax.random.normal(key, shape, jnp.float32) * deviation * level
    return jnp.minimum(jnp.maximum(values, -reach), reach).astype(kind)


def setup_inputs(seed: int = 0) -> dict:
    streams_of = jax.random.split(jax.random.key(seed), 5)
    volume = gaussian(streams_of[0], (VOLS, SIDE_X, SIDE_Y, DEPTH, C_IN), 1.0, 6.0, ((1, 8), (2, 16)))
    w_first = gaussian(streams_of[1], (3, 3, 3, C_IN, C_MID), (27 * C_IN) ** -0.5, 0.109375, ((4, 16),))
    w_second = gaussian(streams_of[2], (3, 3, 3, C_MID, C_OUT), (27 * C_MID) ** -0.5, 0.078125, ((4, 16),))
    cotangent = gaussian(streams_of[3], (VOLS, SIDE_X // 4, SIDE_Y // 4, DEPTH // 4, C_OUT), 1.0, 6.0, ((1, 8), (4, 16)))
    return dict(volume=volume, w_first=w_first, w_second=w_second, cotangent=cotangent)


def pad_low(field):
    return jnp.pad(field, ((0, 0), (1, 0), (1, 0), (1, 0), (0, 0)))

def tap_slice(padded, i, j, k, out_a, out_b, out_c):
    return padded[:, i:i + 2 * out_a:2, j:j + 2 * out_b:2, k:k + 2 * out_c:2, :]

def conv_forward(padded, filters):
    out_a = (padded.shape[1] - 1) // 2
    out_b = (padded.shape[2] - 1) // 2
    out_c = (padded.shape[3] - 1) // 2
    total = jnp.zeros((padded.shape[0], out_a, out_b, out_c, filters.shape[4]), jnp.float32)
    for i in range(3):
        for j in range(3):
            for k in range(3):
                piece = tap_slice(padded, i, j, k, out_a, out_b, out_c)
                total = total + jnp.dot(piece, filters[i, j, k], preferred_element_type=jnp.float32)
    return total

def filter_grad(padded, grad_cells):
    out_a, out_b, out_c = (grad_cells.shape[1], grad_cells.shape[2], grad_cells.shape[3])
    flat_grad = grad_cells.reshape(-1, grad_cells.shape[4])
    rows_all = []
    for i in range(3):
        rows_j = []
        for j in range(3):
            rows_k = []
            for k in range(3):
                piece = tap_slice(padded, i, j, k, out_a, out_b, out_c).reshape(-1, padded.shape[4])
                rows_k.append(jnp.dot(piece.T, flat_grad, preferred_element_type=jnp.float32))
            rows_j.append(jnp.stack(rows_k))
        rows_all.append(jnp.stack(rows_j))
    return jnp.stack(rows_all)

def input_grad_trim(grad_cells, filters):
    count, out_a, out_b, out_c = (grad_cells.shape[0], grad_cells.shape[1], grad_cells.shape[2], grad_cells.shape[3])
    grad_high = jnp.pad(grad_cells, ((0, 0), (0, 1), (0, 1), (0, 1), (0, 0)))
    parity_taps = [[(1, 0)], [(0, 1), (2, 0)]]
    result = jnp.zeros((count, 2 * out_a, 2 * out_b, 2 * out_c, filters.shape[3]), jnp.float32)
    for s_one in range(2):
        for s_two in range(2):
            for s_three in range(2):
                total = jnp.zeros((count, out_a, out_b, out_c, filters.shape[3]), jnp.float32)
                for i, d_one in parity_taps[s_one]:
                    for j, d_two in parity_taps[s_two]:
                        for k, d_three in parity_taps[s_three]:
                            piece = grad_high[:, d_one:d_one + out_a, d_two:d_two + out_b, d_three:d_three + out_c, :]
                            total = total + jnp.dot(piece, filters[i, j, k].T, preferred_element_type=jnp.float32)
                result = result.at[:, s_one::2, s_two::2, s_three::2, :].set(total)
    return result

def reference(volume, w_first, w_second, cotangent):
    vol_pad = pad_low(volume)
    pre_first = conv_forward(vol_pad, w_first)
    hidden_act = jnp.where(pre_first > 0, pre_first, 0.3 * pre_first).astype(jnp.bfloat16)
    act_pad = pad_low(hidden_act)
    second_out = conv_forward(act_pad, w_second).astype(jnp.bfloat16)
    second_grad = filter_grad(act_pad, cotangent)
    act_back = input_grad_trim(cotangent, w_second)
    pre_back = (act_back * jnp.where(pre_first > 0, 1.0, 0.3)).astype(jnp.bfloat16)
    first_grad = filter_grad(vol_pad, pre_back)
    volume_grad = input_grad_trim(pre_back, w_first).astype(jnp.bfloat16)
    return (second_out, volume_grad, first_grad, second_grad)
```

```python
import jax
import jax.numpy as jnp
from jax import lax
from jax.experimental import pallas as pl
from jax.experimental.pallas import tpu as pltpu
from jax.sharding import Mesh
from jax.sharding import PartitionSpec as P

MESH = pl.DeviceIdType.MESH
BF = jnp.bfloat16
F32 = jnp.float32
NSEM = 128

SLOT = {}
for _g in range(9):
    _base = 2 * _g if _g < 5 else 14 + 2 * (_g - 5)
    SLOT[3 * _g + 1], SLOT[3 * _g + 2] = _base, _base + 1
    SLOT[3 * _g] = 10 + _g if _g < 4 else 22 + (_g - 4)


def slot(tap):
    return divmod(SLOT[tap], 14)


def uses(cell, count):
    return [(o, cell - 2 * o) for o in range(count) if 0 <= cell - 2 * o <= 2]


PARITY = (((1, 0),), ((0, 1), (2, 0)))


def dot(a, b):
    return lax.dot_general(a, b, (((1,), (0,)), ((), ())), preferred_element_type=F32)


def dot_nt(a, b):
    return lax.dot_general(a, b, (((1,), (1,)), ((), ())), preferred_element_type=F32)


def loop(count, body):
    def step(i, carry):
        body(i)
        return carry

    lax.fori_loop(0, count, step, 0)


def kernel(
    vol, w1, w2, cotl, so, vg, g1, g2,
    xv, im1, im2, wf1, wf2, w1o, w2o, pre, ab, hid, pb0, pb1, pbt, cott, cot0, cot1, fa, fb, vs,
    g1o, g1s, g1r, c1, r1a, r1b, s1a, s1b, q1a, q1b, t1, y1, f1,
    g2o, g2s, g2r, c2, r2a, r2b, s2a, s2b, q2a, q2b, t2, y2, f2,
    ot, sor, ssem, rsem, lsem,
):
    y, core = lax.axis_index("y"), lax.axis_index("core")
    z, x = lax.axis_index("z"), lax.axis_index("x")
    chan = z * 4 + x
    space = y * 2 + core
    sib = {"core": 1 - core}

    def along(name, me, off):
        return {name: lax.rem(me + off, 4)}

    def chan_at(off):
        c = lax.rem(chan + off, 16)
        return {"z": lax.div(c, 4), "x": lax.rem(c, 4)}

    def space_at(off):
        s = lax.rem(space + off, 8)
        return {"y": lax.div(s, 2), "core": lax.rem(s, 2)}

    sent = []

    def put(src, dst, dev):
        n = len(sent)
        copy = pltpu.make_async_remote_copy(
            src_ref=src, dst_ref=dst, send_sem=ssem.at[n], recv_sem=rsem.at[n],
            device_id=dev, device_id_type=MESH,
        )
        copy.start()
        sent.append(copy)
        return copy

    def arrived(copies):
        for copy in copies:
            copy.wait_recv()

    local = pltpu.make_async_copy(vol, xv.at[:, 1:9, 1:5], lsem.at[0])
    local.start()

    for tap in range(27):
        h, l = slot(tap)
        w1o[h, :, l * 128 : (l + 1) * 128] = w1[tap]
        w2o[h, :, l * 256 : (l + 1) * 256] = w2[tap]
    w1o[1, :, 13 * 128 :] = jnp.zeros((16, 128), BF)
    w2o[1, :, 13 * 256 :] = jnp.zeros((16, 256), BF)
    wf1[core, z, x] = w1o[core]
    wf2[core, z, x] = w2o[core]

    barrier = pltpu.get_barrier_semaphore()
    partners = [chan_at(o) for o in range(1, 16)]
    partners += [along("y", y, o) for o in range(1, 4)]
    partners += [sib, {"y": lax.rem(y + 3 + 2 * core, 4), "core": 1 - core}]
    partners += [{**space_at(1), **chan_at(1)}, {**space_at(7), **chan_at(15)}]
    for dev in partners:
        pl.semaphore_signal(barrier, inc=1, device_id=dev, device_id_type=MESH)
    pl.semaphore_wait(barrier, len(partners))

    def spread_first(own, full, q):
        a = [put(own.at[core, :, pl.ds(0, q)], full.at[core, z, x, :, pl.ds(0, q)], along("x", x, o)) for o in (1, 2, 3)]
        b = [put(own.at[core, :, pl.ds(q, q)], full.at[core, z, x, :, pl.ds(q, q)], along("z", z, o)) for o in (1, 2, 3)]
        return a, b

    def spread_second(full, q, first):
        arrived(first[0])
        part = full.at[core, z, :, :, pl.ds(0, q)]
        a = [put(part, part, along("z", z, o)) for o in (1, 2, 3)]
        arrived(first[1])
        part = full.at[core, :, x, :, pl.ds(q, q)]
        b = [put(part, part, along("x", x, o)) for o in (1, 2, 3)]
        return a, b

    def spread_third(full, second):
        arrived(second[0])
        arrived(second[1])
        return put(full.at[core], full.at[core], sib)

    w1_first = spread_first(w1o, wf1, 896)
    vol_halo = [
        put(vol.at[:, :, 3], xv.at[:, 1:9, 0], chan_at(1)),
        put(vol.at[:, 7], xv.at[:, 0, 1:5], space_at(1)),
        put(vol.at[:, 7, 3], xv.at[:, 0, 0], {**space_at(1), **chan_at(1)}),
    ]
    w2_first = spread_first(w2o, wf2, 1792)
    cots = []
    for o in range(1, 16):
        dev = chan_at(o)
        row = dev["z"] * 4 + dev["x"]
        cots.append(put(cotl.at[pl.ds(row, 2)], cott.at[:, chan], dev))
    cott[:, chan] = cotl[pl.ds(chan, 2)]

    fa[:, 0:8, :] = jnp.zeros((5, 8, 128), F32)
    fb[:, 0:8, :] = jnp.zeros((5, 8, 256), F32)

    def patches(blocks):
        def body(v):
            for a, b in blocks:
                fa[b, 8:72, :] = xv[v, a, b].astype(F32)
                parts = [fa[b, pl.ds(7 + k, 32, 2), :].astype(BF) for k in range(3)]
                for p, i in uses(a, 4):
                    for q, j in uses(b, 2):
                        for k in range(3):
                            h, l = slot(9 * i + 3 * j + k)
                            im1[h, q, p, v, :, l * 128 : (l + 1) * 128] = parts[k]

        loop(4, body)

    def blank(v):
        for q in range(2):
            for p in range(4):
                im1[1, q, p, v, :, 13 * 128 :] = jnp.zeros((32, 128), BF)

    loop(4, blank)
    im2[1, :, :, :, 13 * 256 :] = jnp.zeros((2, 4, 16, 256), BF)
    local.wait()
    patches([(a, b) for a in range(1, 9) for b in range(1, 5)])

    w1_second = spread_second(wf1, 896, w1_first)
    w2_second = spread_second(wf2, 1792, w2_first)

    arrived(cots)
    last = lax.broadcasted_iota(jnp.int32, (64, 256), 0) % 16 == 15
    for b in range(2):
        rows = cott[b].reshape(256, 128).astype(F32).T.astype(BF)
        cot0[b, 0:2] = rows.reshape(2, 4, 16, 256)
    cot_halo = put(cot0.at[:, 0], cot0.at[:, 2], space_at(7))

    arrived(vol_halo)

    @pl.when(chan == 0)
    def _():
        xv[:, :, 0] = jnp.zeros((4, 9, 64, 128), BF)

    @pl.when(space == 0)
    def _():
        xv[:, 0] = jnp.zeros((4, 5, 64, 128), BF)

    patches([(a, 0) for a in range(9)] + [(0, b) for b in range(1, 5)])

    w1_third = spread_third(wf1, w1_second)
    arrived([w1_third])

    def conv_first(q):
        def body(n):
            total = jnp.zeros((256, 256), F32)
            for h in range(2):
                total += dot_nt(im1[h, q, pl.ds(2 * n, 2)].reshape(256, 1792), wf1[h].reshape(256, 1792))
            pre[q, pl.ds(2 * n, 2)] = total.reshape(2, 4, 32, 256)
            act = jnp.where(total > 0, total, 0.3 * total).astype(BF)
            hid[q + 1, pl.ds(2 * n + 1, 2)] = act.reshape(2, 4, 32, 256)

        loop(2, body)

    conv_first(1)
    hid_halo = [
        put(hid.at[2, 1:5], hid.at[0, 1:5], chan_at(1)),
        put(hid.at[2, 4], hid.at[0, 0], {**space_at(1), **chan_at(1)}),
    ]
    w2_third = spread_third(wf2, w2_second)
    conv_first(0)
    hid_halo.append(put(hid.at[1:3, 4], hid.at[1:3, 0], space_at(1)))

    arrived([cot_halo])

    @pl.when(space == 7)
    def _():
        cot0[:, 2] = jnp.zeros((2, 4, 16, 256), BF)

    for b in range(2):
        for a in range(3):
            rows = cot0[b, a].reshape(64, 256).astype(F32)
            rows = jnp.where(last, 0.0, pltpu.roll(rows, 63, 0))
            cot1[b, a] = rows.astype(BF).reshape(4, 16, 256)

    arrived([w2_third])

    cot_at = (cot0, cot1)
    for s1 in range(2):
        for s2 in range(2):
            for s3 in range(2):
                total = jnp.zeros((128, 256), F32)
                for i, d1 in PARITY[s1]:
                    for j, d2 in PARITY[s2]:
                        for k, d3 in PARITY[s3]:
                            h, l = slot(9 * i + 3 * j + k)
                            total += dot(
                                cot_at[d3][d2, d1 : d1 + 2].reshape(128, 256),
                                wf2[h, :, :, :, l * 256 : (l + 1) * 256].reshape(256, 256),
                            )
                for a in range(2):
                    for v in range(4):
                        n = (a * 4 + v) * 16
                        for t in range(2):
                            ab[s2, 2 * a + s1, v, t, pl.ds(s3, 16, 2), :] = total[n : n + 16, t * 128 : (t + 1) * 128]

    def back(q):
        for p in range(4):
            slope = jnp.where(pre[q, p] > 0, 1.0, 0.3)
            act_back = jnp.concatenate([ab[q, p, :, 0], ab[q, p, :, 1]], axis=-1)
            rows = act_back * slope
            pb0[q, p] = rows.astype(BF)
            pbt[q, p] = rows.reshape(128, 256).T.astype(BF)

    loop(2, back)
    pb_halo = [
        put(pb0.at[0, 0:4], pb0.at[2, 0:4], chan_at(15)),
        put(pb0.at[0:2, 0], pb0.at[0:2, 4], space_at(7)),
        put(pb0.at[0, 0], pb0.at[2, 4], {**space_at(7), **chan_at(15)}),
    ]

    def first_filters(half, dst, kind):
        lhs = jnp.concatenate([pbt[q, p] for q in range(2) for p in range(4)], axis=1)

        def body(n):
            at = pl.ds(pl.multiple_of(n * 256, 256), 256)
            dst[:, at] = dot(lhs, im1[half, :, :, :, :, at].reshape(1024, 256)).astype(kind)

        loop(7, body)

    first_filters(1 - core, g1s, BF)
    g1_pair = put(g1s, g1r, sib)
    first_filters(core, g1o, F32)

    arrived(hid_halo)

    @pl.when(chan == 0)
    def _():
        hid[0] = jnp.zeros((5, 4, 32, 256), BF)

    @pl.when(space == 0)
    def _():
        hid[:, 0] = jnp.zeros((3, 4, 32, 256), BF)

    def hidden_patches(v):
        for p in range(5):
            for j in range(3):
                fill = hid[j, p, v].astype(F32)
                parts = []
                for t in range(2):
                    fa[p, 8:40, :] = fill[:, t * 128 : (t + 1) * 128]
                    parts.append([fa[p, pl.ds(7 + k, 16, 2), :].astype(BF) for k in range(3)])
                for a, i in uses(p, 2):
                    for k in range(3):
                        h, l = slot(9 * i + 3 * j + k)
                        for t in range(2):
                            im2[h, a, v, :, l * 256 + t * 128 : l * 256 + (t + 1) * 128] = parts[t][k]

    loop(4, hidden_patches)

    def second_filters(half, dst, kind):
        lhs = cott[0].reshape(256, 128)

        def body(n):
            at = pl.ds(pl.multiple_of(n * 512, 512), 512)
            dst[:, at] = dot(lhs, im2[half, :, :, :, at].reshape(128, 512)).astype(kind)

        loop(7, body)

    second_filters(1 - core, g2s, BF)
    g2_pair = put(g2s, g2r, sib)
    second_filters(core, g2o, F32)

    def sum_pair(pair, own, other, chip, q):
        arrived([pair])

        def body(n):
            at = pl.ds(pl.multiple_of(n * 16, 16), 16)
            total = own[at] + other[at].astype(F32)
            chip[lax.div(n, 4), lax.rem(n, 4)] = total.astype(BF)

        loop(16, body)

    def sum_first(chip, ra, rb, q):
        a, b = [], []
        for o in (1, 2, 3):
            to = lax.rem(z + o, 4)
            a.append(put(chip.at[to, :, :, pl.ds(0, q)], ra.at[o - 1], {"z": to}))
            to = lax.rem(x + o, 4)
            b.append(put(chip.at[:, to, :, pl.ds(q, q)], rb.at[o - 1], {"x": to}))
        return a, b

    def sum_second(chip, ra, rb, sa, sb, qa, qb, q, first):
        arrived(first[0])
        total = chip[z, :, :, 0:q].astype(F32)
        for o in range(3):
            total += ra[o].astype(F32)
        sa[...] = total.astype(BF)
        a, b = [], []
        for o in (1, 2, 3):
            to = lax.rem(x + o, 4)
            a.append(put(sa.at[to], qa.at[o - 1], {"x": to}))
        arrived(first[1])
        total = chip[:, x, :, q : 2 * q].astype(F32)
        for o in range(3):
            total += rb[o].astype(F32)
        sb[...] = total.astype(BF)
        for o in (1, 2, 3):
            to = lax.rem(z + o, 4)
            b.append(put(sb.at[to], qb.at[o - 1], {"z": to}))
        return a, b

    def sum_third(sa, sb, qa, qb, t, yr, q, second):
        arrived(second[0])
        total = sa[x].astype(F32)
        for o in range(3):
            total += qa[o].astype(F32)
        t[:, 0:q] = total.astype(BF)
        arrived(second[1])
        total = sb[z].astype(F32)
        for o in range(3):
            total += qb[o].astype(F32)
        t[:, q : 2 * q] = total.astype(BF)
        return [put(t, yr.at[o - 1], along("y", y, o)) for o in (1, 2, 3)]

    def sum_last(t, yr, f, third):
        arrived(third)
        total = t[...].astype(F32)
        for o in range(3):
            total += yr[o].astype(F32)
        f[core] = total
        return put(f.at[core], f.at[core], sib)

    sum_pair(g1_pair, g1o, g1r, c1, 896)
    g1_first = sum_first(c1, r1a, r1b, 896)

    total = jnp.zeros((256, 128), F32)
    for h in range(2):
        total += dot_nt(wf2[h].reshape(256, 3584), im2[h].reshape(128, 3584))
    ot[...] = total.astype(BF).reshape(16, 16, 128)
    outs = []
    for o in range(1, 16):
        dev = chan_at(o)
        outs.append(put(ot.at[dev["z"] * 4 + dev["x"]], sor.at[chan], dev))
    sor[chan] = ot[chan]

    sum_pair(g2_pair, g2o, g2r, c2, 1792)
    g2_first = sum_first(c2, r2a, r2b, 1792)

    arrived(pb_halo)

    @pl.when(chan == 15)
    def _():
        pb0[2] = jnp.zeros((5, 4, 32, 256), BF)

    @pl.when(space == 7)
    def _():
        pb0[:, 4] = jnp.zeros((3, 4, 32, 256), BF)

    edge = lax.broadcasted_iota(jnp.int32, (128, 256), 0) % 32 == 31

    def shifted(q):
        for p in range(5):
            rows = pb0[q, p].reshape(128, 256).astype(F32)
            rows = jnp.where(edge, 0.0, pltpu.roll(rows, 127, 0))
            pb1[q, p] = rows.astype(BF).reshape(4, 32, 256)

    loop(3, shifted)
    g1_second = sum_second(c1, r1a, r1b, s1a, s1b, q1a, q1b, 896, g1_first)

    def volume_grad(q):
        def body(n):
            for s1 in range(2):
                for s2 in range(2):
                    total = jnp.zeros((256, 256), F32)
                    extra = jnp.zeros((256, 128), F32)
                    for i, d1 in PARITY[s1]:
                        for j, d2 in PARITY[s2]:
                            h, l = slot(9 * i + 3 * j + 1)
                            total += dot(
                                pb0[q + d2, pl.ds(2 * n + d1, 2)].reshape(256, 256),
                                wf1[h, :, :, :, l * 128 : (l + 2) * 128].reshape(256, 256),
                            )
                            h, l = slot(9 * i + 3 * j)
                            extra += dot(
                                pb1[q + d2, pl.ds(2 * n + d1, 2)].reshape(256, 256),
                                wf1[h, :, :, :, l * 128 : (l + 1) * 128].reshape(256, 128),
                            )
                    extra += total[:, 128:]
                    for p in range(2):
                        for v in range(4):
                            m = (p * 4 + v) * 32
                            vs[p * 4 + v, pl.ds(0, 32, 2), :] = total[m : m + 32, 0:128]
                            vs[p * 4 + v, pl.ds(1, 32, 2), :] = extra[m : m + 32]
                            vg[v, 4 * n + 2 * p + s1, 2 * q + s2] = vs[p * 4 + v].astype(BF)

        loop(2, body)

    volume_grad(0)
    g1_third = sum_third(s1a, s1b, q1a, q1b, t1, y1, 896, g1_second)
    g2_second = sum_second(c2, r2a, r2b, s2a, s2b, q2a, q2b, 1792, g2_first)
    volume_grad(1)
    g1_last = sum_last(t1, y1, f1, g1_third)
    g2_third = sum_third(s2a, s2b, q2a, q2b, t2, y2, 1792, g2_second)
    arrived(outs)
    so[...] = sor[...]
    arrived([g1_last])
    for tap in range(27):
        h, l = slot(tap)
        g1[tap] = f1[h, :, l * 128 : (l + 1) * 128]
    g2_last = sum_last(t2, y2, f2, g2_third)
    arrived([g2_last])
    for tap in range(27):
        h, l = slot(tap)
        g2[tap] = f2[h, :, l * 256 : (l + 1) * 256]
    for copy in sent:
        copy.wait_send()


def sums(q):
    return [
        pltpu.VMEM((256, 2 * q), F32),
        pltpu.VMEM((256, 2 * q), BF),
        pltpu.VMEM((256, 2 * q), BF),
        pltpu.VMEM((4, 4, 16, 2 * q), BF),
        pltpu.VMEM((3, 4, 16, q), BF),
        pltpu.VMEM((3, 4, 16, q), BF),
        pltpu.VMEM((4, 16, q), BF),
        pltpu.VMEM((4, 16, q), BF),
        pltpu.VMEM((3, 16, q), BF),
        pltpu.VMEM((3, 16, q), BF),
        pltpu.VMEM((16, 2 * q), BF),
        pltpu.VMEM((3, 16, 2 * q), BF),
        pltpu.VMEM((2, 16, 2 * q), F32),
    ]


def local(volume, w_first, w_second, cotangent):
    w1 = jnp.swapaxes(w_first, 3, 4).reshape(27, 16, 128)
    w2 = jnp.swapaxes(w_second, 3, 4).reshape(27, 16, 256)
    cotl = jnp.transpose(cotangent, (2, 4, 1, 0, 3)).reshape(16, 16, 128)
    cotl = jnp.pad(cotl, ((0, 1), (0, 0), (0, 0)))
    vmem = pl.BlockSpec(memory_space=pltpu.VMEM)
    so, vg, g1, g2 = pl.pallas_call(
        kernel,
        out_shape=(
            jax.ShapeDtypeStruct((16, 16, 128), BF),
            jax.ShapeDtypeStruct((4, 8, 4, 64, 128), BF),
            jax.ShapeDtypeStruct((27, 16, 128), F32),
            jax.ShapeDtypeStruct((27, 16, 256), F32),
        ),
        in_specs=[pl.BlockSpec(memory_space=pl.ANY), vmem, vmem, vmem],
        out_specs=(vmem, vmem, vmem, vmem),
        scratch_shapes=[
            pltpu.VMEM((4, 9, 5, 64, 128), BF),
            pltpu.VMEM((2, 2, 4, 4, 32, 1792), BF),
            pltpu.VMEM((2, 2, 4, 16, 3584), BF),
            pltpu.VMEM((2, 4, 4, 16, 1792), BF),
            pltpu.VMEM((2, 4, 4, 16, 3584), BF),
            pltpu.VMEM((2, 16, 1792), BF),
            pltpu.VMEM((2, 16, 3584), BF),
            pltpu.VMEM((2, 4, 4, 32, 256), F32),
            pltpu.VMEM((2, 4, 4, 2, 32, 128), F32),
            pltpu.VMEM((3, 5, 4, 32, 256), BF),
            pltpu.VMEM((3, 5, 4, 32, 256), BF),
            pltpu.VMEM((3, 5, 4, 32, 256), BF),
            pltpu.VMEM((2, 4, 256, 128), BF),
            pltpu.VMEM((2, 16, 16, 128), BF),
            pltpu.VMEM((2, 3, 4, 16, 256), BF),
            pltpu.VMEM((2, 3, 4, 16, 256), BF),
            pltpu.VMEM((5, 72, 128), F32),
            pltpu.VMEM((5, 40, 256), F32),
            pltpu.VMEM((8, 64, 128), F32),
            *sums(896),
            *sums(1792),
            pltpu.VMEM((16, 16, 128), BF),
            pltpu.VMEM((16, 16, 128), BF),
            pltpu.SemaphoreType.DMA((NSEM,)),
            pltpu.SemaphoreType.DMA((NSEM,)),
            pltpu.SemaphoreType.DMA((1,)),
        ],
        compiler_params=pltpu.CompilerParams(
            collective_id=0, has_side_effects=True, vmem_limit_bytes=60 * 1024 * 1024
        ),
        cost_estimate=pl.CostEstimate(flops=6_800_000_000, bytes_accessed=6_000_000, transcendentals=0),
        name="two_layers",
    )(volume, w1, w2, cotl)
    so = jnp.transpose(so.reshape(16, 16, 2, 4, 16), (3, 2, 0, 4, 1))
    g1 = jnp.swapaxes(g1.reshape(3, 3, 3, 16, 128), 3, 4)
    g2 = jnp.swapaxes(g2.reshape(3, 3, 3, 16, 256), 3, 4)
    return so, vg, g1, g2


def solution(mesh):
    space, chan = ("y", "core"), ("z", "x")
    finer = Mesh(mesh.devices.reshape(4, 2, 4, 4), (*space, *chan))
    return jax.shard_map(
        local,
        mesh=finer,
        in_specs=(
            P(None, space, chan, None, None),
            P(None, None, None, None, chan),
            P(None, None, None, None, chan),
            P(None, space, None, None, chan),
        ),
        out_specs=(
            P(None, space, None, None, chan),
            P(None, space, chan, None, None),
            P(None, None, None, None, chan),
            P(None, None, None, None, chan),
        ),
        check_vma=False,
    )
```

```python
import jax
import jax.numpy as jnp
from jax import lax
from jax.experimental import pallas as pl
from jax.experimental.pallas import tpu as pltpu
from jax.sharding import Mesh
from jax.sharding import PartitionSpec as P

MESH = pl.DeviceIdType.MESH
BF = jnp.bfloat16
F32 = jnp.float32
NSEM = 160

SLOT = {}
for _g in range(9):
    _base = 2 * _g if _g < 5 else 14 + 2 * (_g - 5)
    SLOT[3 * _g + 1], SLOT[3 * _g + 2] = _base, _base + 1
    SLOT[3 * _g] = 10 + _g if _g < 4 else 22 + (_g - 4)


def slot(tap):
    return divmod(SLOT[tap], 14)


def uses(cell, count):
    return [(o, cell - 2 * o) for o in range(count) if 0 <= cell - 2 * o <= 2]


PARITY = (((1, 0),), ((0, 1), (2, 0)))


def dot(a, b):
    return lax.dot_general(a, b, (((1,), (0,)), ((), ())), preferred_element_type=F32)


def dot_nt(a, b):
    return lax.dot_general(a, b, (((1,), (1,)), ((), ())), preferred_element_type=F32)


def loop(count, body):
    def step(i, carry):
        body(i)
        return carry

    lax.fori_loop(0, count, step, 0)


def kernel(
    vol, w1, w2, cot, so, vg, g1, g2,
    xv, im1, im2, wf1, wf2, w1o, w2o, pre, ab, hid, pb0, pb1, pbt, cotv, cotl, cott, cot0, cot1, fa, vs,
    *rest,
):
    sums1, sums2 = rest[:NSUM], rest[NSUM : 2 * NSUM]
    ot, relay, ssem, rsem, lsem, hsend, hrecv = rest[2 * NSUM :]
    y, core = lax.axis_index("y"), lax.axis_index("core")
    z, x = lax.axis_index("z"), lax.axis_index("x")
    chan = z * 4 + x
    space = y * 2 + core
    sib = {"core": 1 - core}

    def along(name, me, off):
        return {name: lax.rem(me + off, 4)}

    def chan_at(off):
        c = lax.rem(chan + off, 16)
        return {"z": lax.div(c, 4), "x": lax.rem(c, 4)}

    def space_at(off):
        s = lax.rem(space + off, 8)
        return {"y": lax.div(s, 2), "core": lax.rem(s, 2)}

    sent = []

    def put(src, dst, dev):
        n = len(sent)
        copy = pltpu.make_async_remote_copy(
            src_ref=src, dst_ref=dst, send_sem=ssem.at[n], recv_sem=rsem.at[n],
            device_id=dev, device_id_type=MESH,
        )
        copy.start()
        sent.append(copy)
        return copy

    class hold:
        def __init__(self, src, dst, dev):
            n = count[0]
            count[0] += 1
            self.send, self.recv = hsend.at[n], hrecv.at[n]
            self.copy = pltpu.make_async_remote_copy(
                src_ref=src, dst_ref=dst, send_sem=self.send, recv_sem=self.recv,
                device_id=dev, device_id_type=MESH,
            )

    count = [0]

    def arrived(copies):
        for copy in copies:
            copy.wait_recv()

    cells = pltpu.make_async_copy(cot, cotv, lsem.at[1])
    cells.start()
    local = pltpu.make_async_copy(vol, xv.at[:, 1:9, 1:5], lsem.at[0])
    local.start()

    barrier = pltpu.get_barrier_semaphore()
    partners = [chan_at(o) for o in range(1, 16)]
    partners += [along("y", y, o) for o in range(1, 4)]
    partners += [sib, {"y": lax.rem(y + 3 + 2 * core, 4), "core": 1 - core}]
    partners += [{**space_at(1), **chan_at(1)}, {**space_at(7), **chan_at(15)}]
    for dev in partners:
        pl.semaphore_signal(barrier, inc=1, device_id=dev, device_id_type=MESH)

    for tap in range(27):
        h, l = slot(tap)
        w1o[h, :, l * 128 : (l + 1) * 128] = w1[tap]
        w2o[h, :, l * 256 : (l + 1) * 256] = w2[tap]
    w1o[1, :, 13 * 128 :] = jnp.zeros((16, 128), BF)
    w2o[1, :, 13 * 256 :] = jnp.zeros((16, 256), BF)
    for own, full, e in ((w1o, wf1, 128), (w2o, wf2, 256)):
        at = pl.ds(pl.multiple_of(y * 2 * e, 2 * e), 2 * e)
        full[core, z, x, :, at] = own[core, :, at]
        full[core, z, x, :, 8 * e :] = own[core, :, 8 * e :]

    pl.semaphore_wait(barrier, len(partners))

    def cut(e):
        q = 2 * e
        return pl.ds(pl.multiple_of(y * q, q), q), pl.ds(8 * e, 4 * e), pl.ds(12 * e, 2 * e)

    def one_row(own, full, at, name):
        me = x if name == "x" else z
        return [put(own.at[core, :, at], full.at[core, z, x, :, at], along(name, me, o)) for o in (1, 2, 3)]

    def four_rows(full, at, name, before):
        arrived(before)
        part = full.at[core, z, :, :, at] if name == "z" else full.at[core, :, x, :, at]
        return [put(part, part, along(name, x if name == "x" else z, o)) for o in (1, 2, 3)]

    def all_rows(full, at, before):
        arrived(before)
        part = full.at[core, :, :, :, at]
        return [put(part, part, along("y", y, o)) for o in (1, 2, 3)]

    def spread_last(full, at, copies):
        arrived(copies)
        part = full.at[core, :, :, :, at]
        return put(part, part, sib)

    (p1, q1, r1), (p2, q2, r2) = cut(128), cut(256)
    w1_px, w1_qx, w1_rz = one_row(w1o, wf1, p1, "x"), one_row(w1o, wf1, q1, "x"), one_row(w1o, wf1, r1, "z")
    w2_px, w2_rz, w2_qx = one_row(w2o, wf2, p2, "x"), one_row(w2o, wf2, r2, "z"), one_row(w2o, wf2, q2, "x")
    vol_plane = put(vol.at[:, 7], xv.at[:, 0, 1:5], space_at(1))

    cells.wait()
    unit = (lax.broadcasted_iota(jnp.int32, (16, 16), 0) == lax.broadcasted_iota(jnp.int32, (16, 16), 1)).astype(BF)
    for b in range(16):
        row = jnp.concatenate([cotv[v, a, b] for a in range(2) for v in range(4)], axis=0)
        cotl[b] = dot_nt(unit, row).astype(BF)
    cotl[16] = jnp.zeros((16, 128), BF)
    cots = []
    for o in range(1, 16):
        dev = chan_at(o)
        row = dev["z"] * 4 + dev["x"]
        cots.append(put(cotl.at[pl.ds(row, 2)], cott.at[:, chan], dev))
    cott[:, chan] = cotl[pl.ds(chan, 2)]

    w1_pz = four_rows(wf1, p1, "z", w1_px)
    w2_pz = four_rows(wf2, p2, "z", w2_px)
    w1_qz = four_rows(wf1, q1, "z", w1_qx)
    w1_rx = four_rows(wf1, r1, "x", w1_rz)

    vol_row = [
        put(vol.at[0:2, :, 3], xv.at[0:2, 1:9, 0], chan_at(1)),
        put(vol.at[:, 7, 3], xv.at[:, 0, 0], {**space_at(1), **chan_at(1)}),
    ]
    vol_step, vol_half = hold(vol.at[2:4, :, 3], relay, {"z": lax.rem(z + 1, 4)}), hold(vol.at[2:4, :, 3], xv.at[2:4, 1:9, 0], chan_at(1))
    vol_on = pltpu.make_async_remote_copy(
        src_ref=relay, dst_ref=xv.at[2:4, 1:9, 0], send_sem=vol_half.send, recv_sem=vol_half.recv,
        device_id=along("x", x, 1), device_id_type=MESH,
    )

    @pl.when(x == 3)
    def _():
        vol_step.copy.start()

    @pl.when(x != 3)
    def _():
        vol_half.copy.start()

    w2_rx = four_rows(wf2, r2, "x", w2_rz)
    w2_qz = four_rows(wf2, q2, "z", w2_qx)

    fa[:, 0:8, :] = jnp.zeros((5, 8, 128), F32)

    def patches(blocks):
        def body(v):
            for a, b in blocks:
                fa[b, 8:72, :] = xv[v, a, b].astype(F32)
                parts = [fa[b, pl.ds(7 + k, 32, 2), :].astype(BF) for k in range(3)]
                for p, i in uses(a, 4):
                    for q, j in uses(b, 2):
                        for k in range(3):
                            h, l = slot(9 * i + 3 * j + k)
                            im1[h, q, p, v, :, l * 128 : (l + 1) * 128] = parts[k]

        loop(4, body)

    def blank(v):
        for q in range(2):
            for p in range(4):
                im1[1, q, p, v, :, 13 * 128 :] = jnp.zeros((32, 128), BF)

    loop(4, blank)
    im2[1, :, :, :, 13 * 256 :] = jnp.zeros((2, 4, 16, 256), BF)
    local.wait()
    patches([(a, b) for a in range(1, 9) for b in range(1, 5)])
    w1_py = all_rows(wf1, p1, w1_pz)
    w2_py = all_rows(wf2, p2, w2_pz)

    @pl.when(x == 3)
    def _():
        vol_step.copy.wait()
        vol_on.start()

    arrived(cots)
    for b in range(2):
        rows = cott[b].reshape(256, 128).astype(F32).T.astype(BF)
        cot0[b, 0:2] = rows.reshape(2, 4, 16, 256)
    cot_halo = put(cot0.at[:, 0], cot0.at[:, 2], space_at(7))

    arrived([vol_plane])

    @pl.when(space == 0)
    def _():
        xv[:, 0, 1:5] = jnp.zeros((4, 4, 64, 128), BF)

    patches([(0, b) for b in range(1, 5)])

    w1_last = [spread_last(wf1, pl.ds(1024, 768), w1_qz + w1_rx), spread_last(wf1, pl.ds(0, 1024), w1_py)]
    arrived(w1_last)

    def conv_first(q):
        def body(n):
            total = jnp.zeros((256, 256), F32)
            for h in range(2):
                total += dot_nt(im1[h, q, pl.ds(2 * n, 2)].reshape(256, 1792), wf1[h].reshape(256, 1792))
            pre[q, pl.ds(2 * n, 2)] = total.reshape(2, 4, 32, 256)
            act = jnp.where(total > 0, total, 0.3 * total).astype(BF)
            hid[q + 1, pl.ds(2 * n + 1, 2)] = act.reshape(2, 4, 32, 256)

        loop(2, body)

    conv_first(1)
    hid_halo = [
        put(hid.at[2, 1:5], hid.at[0, 1:5], chan_at(1)),
        put(hid.at[2, 4], hid.at[0, 0], {**space_at(1), **chan_at(1)}),
    ]

    arrived([cot_halo])

    @pl.when(space == 7)
    def _():
        cot0[:, 2] = jnp.zeros((2, 4, 16, 256), BF)

    last = lax.broadcasted_iota(jnp.int32, (64, 256), 0) % 16 == 15
    for b in range(2):
        for a in range(3):
            rows = cot0[b, a].reshape(64, 256).astype(F32)
            rows = jnp.where(last, 0.0, pltpu.roll(rows, 63, 0))
            cot1[b, a] = rows.astype(BF).reshape(4, 16, 256)

    arrived(vol_row)
    vol_half.copy.wait_recv()

    @pl.when(chan == 0)
    def _():
        xv[:, :, 0] = jnp.zeros((4, 9, 64, 128), BF)

    @pl.when(space == 0)
    def _():
        xv[:, 0, 0] = jnp.zeros((4, 64, 128), BF)

    patches([(a, 0) for a in range(9)])
    conv_first(0)
    hid_halo.append(put(hid.at[1:3, 4], hid.at[1:3, 0], space_at(1)))
    w2_last = [spread_last(wf2, pl.ds(2048, 1536), w2_qz + w2_rx), spread_last(wf2, pl.ds(0, 2048), w2_py)]
    arrived(w2_last)

    cot_at = (cot0, cot1)
    for s1 in range(2):
        for s2 in range(2):
            for s3 in range(2):
                total = jnp.zeros((128, 256), F32)
                for i, d1 in PARITY[s1]:
                    for j, d2 in PARITY[s2]:
                        for k, d3 in PARITY[s3]:
                            h, l = slot(9 * i + 3 * j + k)
                            total += dot(
                                cot_at[d3][d2, d1 : d1 + 2].reshape(128, 256),
                                wf2[h, :, :, :, l * 256 : (l + 1) * 256].reshape(256, 256),
                            )
                for a in range(2):
                    for v in range(4):
                        n = (a * 4 + v) * 16
                        for t in range(2):
                            ab[s2, 2 * a + s1, v, t, pl.ds(s3, 16, 2), :] = total[n : n + 16, t * 128 : (t + 1) * 128]

    def back(q):
        for p in range(4):
            slope = jnp.where(pre[q, p] > 0, 1.0, 0.3)
            act_back = jnp.concatenate([ab[q, p, :, 0], ab[q, p, :, 1]], axis=-1)
            rows = act_back * slope
            pb0[q, p] = rows.astype(BF)
            pbt[q, p] = rows.reshape(128, 256).T.astype(BF)

    loop(2, back)
    pb_halo = [
        put(pb0.at[0, 0:4], pb0.at[2, 0:4], chan_at(15)),
        put(pb0.at[0:2, 0], pb0.at[0:2, 4], space_at(7)),
        put(pb0.at[0, 0], pb0.at[2, 4], {**space_at(7), **chan_at(15)}),
    ]

    arrived(hid_halo)

    @pl.when(chan == 0)
    def _():
        hid[0] = jnp.zeros((5, 4, 32, 256), BF)

    @pl.when(space == 0)
    def _():
        hid[:, 0] = jnp.zeros((3, 4, 32, 256), BF)

    def hidden_patches(v):
        for p in range(5):
            for j in range(3):
                fill = hid[j, p, v].astype(F32)
                parts = []
                for t in range(2):
                    fa[p, 8:40, :] = fill[:, t * 128 : (t + 1) * 128]
                    parts.append([fa[p, pl.ds(7 + k, 16, 2), :].astype(BF) for k in range(3)])
                for a, i in uses(p, 2):
                    for k in range(3):
                        h, l = slot(9 * i + 3 * j + k)
                        for t in range(2):
                            im2[h, a, v, :, l * 256 + t * 128 : l * 256 + (t + 1) * 128] = parts[t][k]

    loop(4, hidden_patches)

    def second_filters(half, dst, kind):
        lhs = cott[0].reshape(256, 128)

        def body(n):
            at = pl.ds(pl.multiple_of(n * 512, 512), 512)
            dst[:, at] = dot(lhs, im2[half, :, :, :, at].reshape(128, 512)).astype(kind)

        loop(7, body)

    def first_filters(half, dst, kind):
        lhs = jnp.concatenate([pbt[q, p] for q in range(2) for p in range(4)], axis=1)

        def body(n):
            at = pl.ds(pl.multiple_of(n * 256, 256), 256)
            dst[:, at] = dot(lhs, im1[half, :, :, :, :, at].reshape(1024, 256)).astype(kind)

        loop(7, body)

    class Sum:
        def __init__(self, refs, e):
            self.e = e
            (self.own, self.out, self.other, self.chip, self.yr, self.ys, self.fin) = refs[:7]
            self.recv = refs[7:10], refs[10:13], refs[13:16]
            self.yq, self.yp, self.full = refs[16:19]
            w = [e, 5 * e, 5 * e]
            self.width = w
            self.begin = [0, 4 * e, 9 * e]
            self.order = "zx", "zx", "xz"

        def pair(self, filters):
            filters(1 - core, self.out, BF)
            self.link = put(self.out, self.other, sib)

        def start(self):
            arrived([self.link])

            def body(n):
                at = pl.ds(pl.multiple_of(n * 16, 16), 16)
                total = self.own[at] + self.other[at].astype(F32)
                self.chip[lax.div(n, 4), lax.rem(n, 4)] = total.astype(BF)

            loop(16, body)
            e = self.e
            self.copies = []
            for o in (1, 2, 3):
                to = lax.rem(y + o, 4)
                at = pl.ds(pl.multiple_of(to * e, e), e)
                self.copies.append(put(self.chip.at[:, :, :, at], self.yr.at[o - 1], {"y": to}))
            self.first = [None, self.send_first(1), self.send_first(2)]

        def source(self, part):
            if part == 0:
                return self.ys, pl.ds(0, self.e)
            return self.chip, pl.ds(self.begin[part], self.width[part])

        def send_first(self, part):
            src, at = self.source(part)
            name, me = ("z", z) if self.order[part][0] == "z" else ("x", x)
            out = []
            for o in (1, 2, 3):
                to = lax.rem(me + o, 4)
                view = src.at[to, :, :, at] if name == "z" else src.at[:, to, :, at]
                out.append(put(view, self.recv[part][0].at[o - 1], {name: to}))
            return out

        def shared(self):
            arrived(self.copies)
            e = self.e
            at = pl.ds(pl.multiple_of(y * e, e), e)

            def body(n):
                total = self.chip[n, :, :, at].astype(F32)
                for o in range(3):
                    total += self.yr[o, n].astype(F32)
                self.ys[n] = total.astype(BF)

            loop(4, body)
            self.first[0] = self.send_first(0)

        def second(self, part):
            arrived(self.first[part])
            src, at = self.source(part)
            got, mid, _ = self.recv[part]
            total = (src[z, :, :, at] if self.order[part][0] == "z" else src[:, x, :, at]).astype(F32)
            for o in range(3):
                total += got[o].astype(F32)
            mid[...] = total.astype(BF)
            name, me = ("x", x) if self.order[part][0] == "z" else ("z", z)
            out = []
            for o in (1, 2, 3):
                to = lax.rem(me + o, 4)
                out.append(put(mid.at[to], self.recv[part][2].at[o - 1], {name: to}))
            self.first[part] = out

        def third(self, part):
            arrived(self.first[part])
            _, mid, got = self.recv[part]
            total = (mid[x] if self.order[part][0] == "z" else mid[z]).astype(F32)
            for o in range(3):
                total += got[o].astype(F32)
            e = self.e
            if part == 0:
                self.fin[y] = total.astype(BF)
                self.last0 = [put(self.fin.at[y], self.fin.at[y], along("y", y, o)) for o in (1, 2, 3)]
            else:
                at = slice((part - 1) * 5 * e, part * 5 * e)
                self.yq[:, at] = total.astype(BF)

        def fourth(self):
            self.last1 = [put(self.yq, self.yp.at[o - 1], along("y", y, o)) for o in (1, 2, 3)]

        def final(self):
            e = self.e
            arrived(self.last0)
            for n in range(4):
                self.full[core, :, n * e : (n + 1) * e] = self.fin[n].astype(F32)
            arrived(self.last1)
            total = self.yq[...].astype(F32)
            for o in range(3):
                total += self.yp[o].astype(F32)
            self.full[core, :, 4 * e : 14 * e] = total
            self.done = put(self.full.at[core], self.full.at[core], sib)

    sum1, sum2 = Sum(sums1, 128), Sum(sums2, 256)
    sum2.pair(second_filters)
    second_filters(core, sum2.own, F32)
    sum1.pair(first_filters)
    sum2.start()
    first_filters(core, sum1.own, F32)
    sum1.start()

    total = jnp.zeros((256, 128), F32)
    for h in range(2):
        total += dot_nt(wf2[h].reshape(256, 3584), im2[h].reshape(128, 3584))
    ot[...] = total.astype(BF).reshape(16, 16, 128)
    outs = []
    for o in range(1, 16):
        dev = chan_at(o)
        outs.append(put(ot.at[dev["z"] * 4 + dev["x"]], so.at[chan], dev))
    so[chan] = ot[chan]
    sum2.shared()

    arrived(pb_halo)

    @pl.when(chan == 15)
    def _():
        pb0[2] = jnp.zeros((5, 4, 32, 256), BF)

    @pl.when(space == 7)
    def _():
        pb0[:, 4] = jnp.zeros((3, 4, 32, 256), BF)

    edge = lax.broadcasted_iota(jnp.int32, (128, 256), 0) % 32 == 31

    def shifted(q):
        for p in range(5):
            rows = pb0[q, p].reshape(128, 256).astype(F32)
            rows = jnp.where(edge, 0.0, pltpu.roll(rows, 127, 0))
            pb1[q, p] = rows.astype(BF).reshape(4, 32, 256)

    loop(3, shifted)

    def volume_grad(q):
        def body(n):
            for s1 in range(2):
                for s2 in range(2):
                    total = jnp.zeros((256, 256), F32)
                    extra = jnp.zeros((256, 128), F32)
                    for i, d1 in PARITY[s1]:
                        for j, d2 in PARITY[s2]:
                            h, l = slot(9 * i + 3 * j + 1)
                            total += dot(
                                pb0[q + d2, pl.ds(2 * n + d1, 2)].reshape(256, 256),
                                wf1[h, :, :, :, l * 128 : (l + 2) * 128].reshape(256, 256),
                            )
                            h, l = slot(9 * i + 3 * j)
                            extra += dot(
                                pb1[q + d2, pl.ds(2 * n + d1, 2)].reshape(256, 256),
                                wf1[h, :, :, :, l * 128 : (l + 1) * 128].reshape(256, 128),
                            )
                    extra += total[:, 128:]
                    for p in range(2):
                        for v in range(4):
                            m = (p * 4 + v) * 32
                            vs[p * 4 + v, pl.ds(0, 32, 2), :] = total[m : m + 32, 0:128]
                            vs[p * 4 + v, pl.ds(1, 32, 2), :] = extra[m : m + 32]
                            vg[v, 4 * n + 2 * p + s1, 2 * q + s2] = vs[p * 4 + v].astype(BF)

        loop(2, body)

    volume_grad(0)
    sum1.shared()
    sum2.second(1)
    sum2.second(2)
    sum2.second(0)
    volume_grad(1)
    sum1.second(1)
    sum1.second(2)
    sum1.second(0)
    for part in (1, 2):
        sum2.third(part)
    sum2.fourth()
    sum2.third(0)
    for part in (1, 2):
        sum1.third(part)
    sum1.fourth()
    sum1.third(0)
    arrived(outs)
    sum2.final()
    sum1.final()
    arrived([sum2.done])
    for h in range(2):
        g2[h] = sum2.full[h]
    arrived([sum1.done])
    for h in range(2):
        g1[h] = sum1.full[h]
    for copy in sent:
        copy.wait_send()
    vol_half.copy.wait_send()


def finish(so, vg, g1, g2, so_out, vg_out, g1_out, g2_out, held, sem):
    loads = [pltpu.make_async_copy(vg.at[v], held.at[v], sem.at[0, v]) for v in range(4)]
    stores = [pltpu.make_async_copy(held.at[v], vg_out.at[v], sem.at[1, v]) for v in range(4)]
    for copy in loads:
        copy.start()
    for v in range(4):
        loads[v].wait()
        stores[v].start()
    rows = so[...].reshape(256, 128).astype(F32).T.astype(BF)
    for b in range(16):
        for a in range(2):
            for v in range(4):
                n = (a * 4 + v) * 16
                so_out[v, a, b] = rows[n : n + 16, 16 * b : 16 * b + 16]
    for tap in range(27):
        h, l = slot(tap)
        g1_out[tap] = g1[h, :, l * 128 : (l + 1) * 128]
        g2_out[tap] = g2[h, :, l * 256 : (l + 1) * 256]
    for copy in stores:
        copy.wait()


NSUM = 19


def sums(e):
    per_part = []
    for width, part in ((e, 0), (5 * e, 1), (5 * e, 2)):
        per_part += [
            pltpu.VMEM((3, 4, 16, width), BF),
            pltpu.VMEM((4, 16, width), BF),
            pltpu.VMEM((3, 16, width), BF),
        ]
    return [
        pltpu.VMEM((256, 14 * e), F32),
        pltpu.VMEM((256, 14 * e), BF),
        pltpu.VMEM((256, 14 * e), BF),
        pltpu.VMEM((4, 4, 16, 14 * e), BF),
        pltpu.VMEM((3, 4, 4, 16, e), BF),
        pltpu.VMEM((4, 4, 16, e), BF),
        pltpu.VMEM((4, 16, e), BF),
        *per_part,
        pltpu.VMEM((16, 10 * e), BF),
        pltpu.VMEM((3, 16, 10 * e), BF),
        pltpu.VMEM((2, 16, 14 * e), F32),
    ]


def local(volume, w_first, w_second, cotangent):
    w1 = jnp.swapaxes(w_first, 3, 4).reshape(27, 16, 128)
    w2 = jnp.swapaxes(w_second, 3, 4).reshape(27, 16, 256)
    vmem, anywhere = pl.BlockSpec(memory_space=pltpu.VMEM), pl.BlockSpec(memory_space=pl.ANY)
    so, vg, g1, g2 = pl.pallas_call(
        kernel,
        out_shape=(
            jax.ShapeDtypeStruct((16, 16, 128), BF),
            jax.ShapeDtypeStruct((4, 8, 4, 64, 128), BF),
            jax.ShapeDtypeStruct((2, 16, 1792), F32),
            jax.ShapeDtypeStruct((2, 16, 3584), F32),
        ),
        in_specs=[anywhere, vmem, vmem, anywhere],
        out_specs=(vmem, vmem, vmem, vmem),
        scratch_shapes=[
            pltpu.VMEM((4, 9, 5, 64, 128), BF),
            pltpu.VMEM((2, 2, 4, 4, 32, 1792), BF),
            pltpu.VMEM((2, 2, 4, 16, 3584), BF),
            pltpu.VMEM((2, 4, 4, 16, 1792), BF),
            pltpu.VMEM((2, 4, 4, 16, 3584), BF),
            pltpu.VMEM((2, 16, 1792), BF),
            pltpu.VMEM((2, 16, 3584), BF),
            pltpu.VMEM((2, 4, 4, 32, 256), F32),
            pltpu.VMEM((2, 4, 4, 2, 32, 128), F32),
            pltpu.VMEM((3, 5, 4, 32, 256), BF),
            pltpu.VMEM((3, 5, 4, 32, 256), BF),
            pltpu.VMEM((3, 5, 4, 32, 256), BF),
            pltpu.VMEM((2, 4, 256, 128), BF),
            pltpu.VMEM((4, 2, 16, 16, 16), BF),
            pltpu.VMEM((17, 16, 128), BF),
            pltpu.VMEM((2, 16, 16, 128), BF),
            pltpu.VMEM((2, 3, 4, 16, 256), BF),
            pltpu.VMEM((2, 3, 4, 16, 256), BF),
            pltpu.VMEM((5, 72, 128), F32),
            pltpu.VMEM((8, 64, 128), F32),
            *sums(128),
            *sums(256),
            pltpu.VMEM((16, 16, 128), BF),
            pltpu.VMEM((2, 8, 64, 128), BF),
            pltpu.SemaphoreType.DMA((NSEM,)),
            pltpu.SemaphoreType.DMA((NSEM,)),
            pltpu.SemaphoreType.DMA((2,)),
            pltpu.SemaphoreType.DMA((2,)),
            pltpu.SemaphoreType.DMA((2,)),
        ],
        compiler_params=pltpu.CompilerParams(
            collective_id=0, has_side_effects=True, vmem_limit_bytes=56 * 1024 * 1024
        ),
        cost_estimate=pl.CostEstimate(flops=6_800_000_000, bytes_accessed=6_000_000, transcendentals=0),
        name="two_layers",
    )(volume, w1, w2, cotangent)
    so, vg, g1, g2 = pl.pallas_call(
        finish,
        out_shape=(
            jax.ShapeDtypeStruct((4, 2, 16, 16, 16), BF),
            jax.ShapeDtypeStruct((4, 8, 4, 64, 128), BF),
            jax.ShapeDtypeStruct((27, 16, 128), F32),
            jax.ShapeDtypeStruct((27, 16, 256), F32),
        ),
        in_specs=[vmem, anywhere, vmem, vmem],
        out_specs=(vmem, anywhere, vmem, vmem),
        scratch_shapes=[pltpu.VMEM((4, 8, 4, 64, 128), BF), pltpu.SemaphoreType.DMA((2, 4))],
        name="finish",
    )(so, vg, g1, g2)
    g1 = jnp.swapaxes(g1.reshape(3, 3, 3, 16, 128), 3, 4)
    g2 = jnp.swapaxes(g2.reshape(3, 3, 3, 16, 256), 3, 4)
    return so, vg, g1, g2


def solution(mesh):
    space, chan = ("y", "core"), ("z", "x")
    finer = Mesh(mesh.devices.reshape(4, 2, 4, 4), (*space, *chan))
    return jax.shard_map(
        local,
        mesh=finer,
        in_specs=(
            P(None, space, chan, None, None),
            P(None, None, None, None, chan),
            P(None, None, None, None, chan),
            P(None, space, None, None, chan),
        ),
        out_specs=(
            P(None, space, None, None, chan),
            P(None, space, chan, None, None),
            P(None, None, None, None, chan),
            P(None, None, None, None, chan),
        ),
        check_vma=False,
    )
```

```python
import jax
import jax.numpy as jnp
from jax import lax
from jax.experimental import pallas as pl
from jax.experimental.pallas import tpu as pltpu
from jax.sharding import Mesh
from jax.sharding import PartitionSpec as P

MESH = pl.DeviceIdType.MESH
BF = jnp.bfloat16
F32 = jnp.float32
NSEM = 160

SLOT = {}
for _g in range(9):
    _base = 2 * _g if _g < 5 else 14 + 2 * (_g - 5)
    SLOT[3 * _g + 1], SLOT[3 * _g + 2] = _base, _base + 1
    SLOT[3 * _g] = 10 + _g if _g < 4 else 22 + (_g - 4)


def slot(tap):
    return divmod(SLOT[tap], 14)


def uses(cell, count):
    return [(o, cell - 2 * o) for o in range(count) if 0 <= cell - 2 * o <= 2]


PARITY = (((1, 0),), ((0, 1), (2, 0)))


def dot(a, b):
    return lax.dot_general(a, b, (((1,), (0,)), ((), ())), preferred_element_type=F32)


def dot_nt(a, b):
    return lax.dot_general(a, b, (((1,), (1,)), ((), ())), preferred_element_type=F32)


def loop(count, body):
    def step(i, carry):
        body(i)
        return carry

    lax.fori_loop(0, count, step, 0)


def kernel(
    vol, w1, w2, cot, so, vg, g1, g2,
    xv, im1, im2, wf1, wf2, w1o, w2o, pre, ab, hid, pb0, pb1, pbt, cotv, cotl, cott, cot0, cot1, fa, vs,
    *rest,
):
    sums1, sums2 = rest[:NSUM], rest[NSUM : 2 * NSUM]
    ot, sor, relay, ssem, rsem, lsem, hsend, hrecv = rest[2 * NSUM :]
    y, core = lax.axis_index("y"), lax.axis_index("core")
    z, x = lax.axis_index("z"), lax.axis_index("x")
    chan = z * 4 + x
    space = y * 2 + core
    sib = {"core": 1 - core}

    def along(name, me, off):
        return {name: lax.rem(me + off, 4)}

    def chan_at(off):
        c = lax.rem(chan + off, 16)
        return {"z": lax.div(c, 4), "x": lax.rem(c, 4)}

    def space_at(off):
        s = lax.rem(space + off, 8)
        return {"y": lax.div(s, 2), "core": lax.rem(s, 2)}

    sent = []

    def put(src, dst, dev):
        n = len(sent)
        copy = pltpu.make_async_remote_copy(
            src_ref=src, dst_ref=dst, send_sem=ssem.at[n], recv_sem=rsem.at[n],
            device_id=dev, device_id_type=MESH,
        )
        copy.start()
        sent.append(copy)
        return copy

    class hold:
        def __init__(self, src, dst, dev):
            n = count[0]
            count[0] += 1
            self.send, self.recv = hsend.at[n], hrecv.at[n]
            self.copy = pltpu.make_async_remote_copy(
                src_ref=src, dst_ref=dst, send_sem=self.send, recv_sem=self.recv,
                device_id=dev, device_id_type=MESH,
            )

    count = [0]

    def arrived(copies):
        for copy in copies:
            copy.wait_recv()

    cells = pltpu.make_async_copy(cot, cotv, lsem.at[1])
    cells.start()
    local = pltpu.make_async_copy(vol, xv.at[:, 1:9, 1:5], lsem.at[0])
    local.start()

    barrier = pltpu.get_barrier_semaphore()
    partners = [chan_at(o) for o in range(1, 16)]
    partners += [along("y", y, o) for o in range(1, 4)]
    partners += [sib, {"y": lax.rem(y + 3 + 2 * core, 4), "core": 1 - core}]
    partners += [{**space_at(1), **chan_at(1)}, {**space_at(7), **chan_at(15)}]
    for dev in partners:
        pl.semaphore_signal(barrier, inc=1, device_id=dev, device_id_type=MESH)

    for tap in range(27):
        h, l = slot(tap)
        w1o[h, :, l * 128 : (l + 1) * 128] = w1[tap]
        w2o[h, :, l * 256 : (l + 1) * 256] = w2[tap]
    w1o[1, :, 13 * 128 :] = jnp.zeros((16, 128), BF)
    w2o[1, :, 13 * 256 :] = jnp.zeros((16, 256), BF)
    for own, full, q, rest_at in ((w1o, wf1, 128, 512), (w2o, wf2, 256, 1024)):
        at = pl.ds(pl.multiple_of(y * q, q), q)
        full[core, z, x, :, at] = own[core, :, at]
        full[core, z, x, :, rest_at:] = own[core, :, rest_at:]

    pl.semaphore_wait(barrier, len(partners))

    def cut(e, shared, direct):
        q = shared // 4 * e
        return (
            pl.ds(pl.multiple_of(y * q, q), q),
            pl.ds(shared * e, direct * e),
            pl.ds((shared + direct) * e, (14 - shared - direct) * e),
        )

    def one_row(own, full, at, name):
        me = x if name == "x" else z
        return [put(own.at[core, :, at], full.at[core, z, x, :, at], along(name, me, o)) for o in (1, 2, 3)]

    def four_rows(full, at, name, before):
        arrived(before)
        part = full.at[core, z, :, :, at] if name == "z" else full.at[core, :, x, :, at]
        return [put(part, part, along(name, x if name == "x" else z, o)) for o in (1, 2, 3)]

    def all_rows(full, at, before):
        arrived(before)
        part = full.at[core, :, :, :, at]
        return [put(part, part, along("y", y, o)) for o in (1, 2, 3)]

    def spread_last(full, at, copies):
        arrived(copies)
        part = full.at[core, :, :, :, at]
        return put(part, part, sib)

    (p1, q1, r1), (p2, q2, r2) = cut(128, 4, 6), cut(256, 4, 6)
    w1_px, w1_qx, w1_rz = one_row(w1o, wf1, p1, "x"), one_row(w1o, wf1, q1, "x"), one_row(w1o, wf1, r1, "z")
    w2_px, w2_rz, w2_qx = one_row(w2o, wf2, p2, "x"), one_row(w2o, wf2, r2, "z"), one_row(w2o, wf2, q2, "x")
    vol_plane = put(vol.at[:, 7], xv.at[:, 0, 1:5], space_at(1))

    cells.wait()
    unit = (lax.broadcasted_iota(jnp.int32, (16, 16), 0) == lax.broadcasted_iota(jnp.int32, (16, 16), 1)).astype(BF)
    for b in range(16):
        row = jnp.concatenate([cotv[v, a, b] for a in range(2) for v in range(4)], axis=0)
        cotl[b] = dot_nt(unit, row).astype(BF)
    cotl[16] = jnp.zeros((16, 128), BF)
    cots = []
    for o in range(1, 16):
        dev = chan_at(o)
        row = dev["z"] * 4 + dev["x"]
        cots.append(put(cotl.at[pl.ds(row, 2)], cott.at[:, chan], dev))
    cott[:, chan] = cotl[pl.ds(chan, 2)]

    w1_pz = four_rows(wf1, p1, "z", w1_px)
    w2_pz = four_rows(wf2, p2, "z", w2_px)
    w1_rx = four_rows(wf1, r1, "x", w1_rz)
    w1_qz = four_rows(wf1, q1, "z", w1_qx)

    vol_row = [
        put(vol.at[0:2, :, 3], xv.at[0:2, 1:9, 0], chan_at(1)),
        put(vol.at[:, 7, 3], xv.at[:, 0, 0], {**space_at(1), **chan_at(1)}),
    ]
    vol_step, vol_half = hold(vol.at[2:4, :, 3], relay, {"z": lax.rem(z + 1, 4)}), hold(vol.at[2:4, :, 3], xv.at[2:4, 1:9, 0], chan_at(1))
    vol_on = pltpu.make_async_remote_copy(
        src_ref=relay, dst_ref=xv.at[2:4, 1:9, 0], send_sem=vol_half.send, recv_sem=vol_half.recv,
        device_id=along("x", x, 1), device_id_type=MESH,
    )

    @pl.when(x == 3)
    def _():
        vol_step.copy.start()

    @pl.when(x != 3)
    def _():
        vol_half.copy.start()

    w2_rx = four_rows(wf2, r2, "x", w2_rz)
    w2_qz = four_rows(wf2, q2, "z", w2_qx)

    fa[:, 0:8, :] = jnp.zeros((5, 8, 128), F32)

    def patches(blocks):
        def body(v):
            for a, b in blocks:
                fa[b, 8:72, :] = xv[v, a, b].astype(F32)
                parts = [fa[b, pl.ds(7 + k, 32, 2), :].astype(BF) for k in range(3)]
                for p, i in uses(a, 4):
                    for q, j in uses(b, 2):
                        for k in range(3):
                            h, l = slot(9 * i + 3 * j + k)
                            im1[h, q, p, v, :, l * 128 : (l + 1) * 128] = parts[k]

        loop(4, body)

    def blank(v):
        for q in range(2):
            for p in range(4):
                im1[1, q, p, v, :, 13 * 128 :] = jnp.zeros((32, 128), BF)

    loop(4, blank)
    im2[1, :, :, :, 13 * 256 :] = jnp.zeros((2, 4, 16, 256), BF)
    local.wait()
    patches([(a, b) for a in range(1, 9) for b in range(1, 5)])
    w1_py = all_rows(wf1, p1, w1_pz)
    w2_py = all_rows(wf2, p2, w2_pz)
    @pl.when(x == 3)
    def _():
        vol_step.copy.wait()
        vol_on.start()

    arrived(cots)
    for b in range(2):
        rows = cott[b].reshape(256, 128).astype(F32).T.astype(BF)
        cot0[b, 0:2] = rows.reshape(2, 4, 16, 256)
    cot_halo = put(cot0.at[:, 0], cot0.at[:, 2], space_at(7))

    arrived([vol_plane])

    @pl.when(space == 0)
    def _():
        xv[:, 0, 1:5] = jnp.zeros((4, 4, 64, 128), BF)

    patches([(0, b) for b in range(1, 5)])

    w1_last = [
        spread_last(wf1, pl.ds(0, 512), w1_py),
        spread_last(wf1, pl.ds(512, 1280), w1_qz + w1_rx),
    ]
    arrived(w1_last)

    def conv_first(q):
        def body(n):
            total = jnp.zeros((256, 256), F32)
            for h in range(2):
                total += dot_nt(im1[h, q, pl.ds(2 * n, 2)].reshape(256, 1792), wf1[h].reshape(256, 1792))
            pre[q, pl.ds(2 * n, 2)] = total.reshape(2, 4, 32, 256)
            act = jnp.where(total > 0, total, 0.3 * total).astype(BF)
            hid[q, pl.ds(2 * n + 1, 2)] = act.reshape(2, 4, 32, 256)

        loop(2, body)

    conv_first(1)

    arrived([cot_halo])

    @pl.when(space == 7)
    def _():
        cot0[:, 2] = jnp.zeros((2, 4, 16, 256), BF)

    last = lax.broadcasted_iota(jnp.int32, (64, 256), 0) % 16 == 15
    for b in range(2):
        for a in range(3):
            rows = cot0[b, a].reshape(64, 256).astype(F32)
            rows = jnp.where(last, 0.0, pltpu.roll(rows, 63, 0))
            cot1[b, a] = rows.astype(BF).reshape(4, 16, 256)

    arrived(vol_row)
    vol_half.copy.wait_recv()

    @pl.when(chan == 0)
    def _():
        xv[:, :, 0] = jnp.zeros((4, 9, 64, 128), BF)

    @pl.when(space == 0)
    def _():
        xv[:, 0, 0] = jnp.zeros((4, 64, 128), BF)

    patches([(a, 0) for a in range(9)])
    conv_first(0)
    hid_halo = [put(hid.at[0:2, 4], hid.at[0:2, 0], space_at(1))]
    w2_last = [spread_last(wf2, pl.ds(0, 1024), w2_py), spread_last(wf2, pl.ds(1024, 2560), w2_qz + w2_rx)]

    def second_filters(half, dst, kind):
        def body(n):
            at = pl.ds(pl.multiple_of(n * 256, 256), 256)
            place = half * 14 + n
            following = jnp.int32(0)
            for tap in range(27):
                if tap // 3 % 3 == 0:
                    following += jnp.where(place == SLOT[tap], 1, 0)
            lhs = cott[following].reshape(256, 128)
            dst[:, at] = dot(lhs, im2[half, :, :, :, at].reshape(128, 256)).astype(kind)

        loop(14, body)

    def first_filters(half, dst, kind):
        lhs = jnp.concatenate([pbt[q, p] for q in range(2) for p in range(4)], axis=1)

        def body(n):
            at = pl.ds(pl.multiple_of(n * 256, 256), 256)
            dst[:, at] = dot(lhs, im1[half, :, :, :, :, at].reshape(1024, 256)).astype(kind)

        loop(7, body)

    class Sum:
        def __init__(self, refs, e):
            self.e = e
            (self.own, self.out, self.other, self.chip, self.yr, self.ys, self.fin) = refs[:7]
            self.recv = refs[7:10], refs[10:13], refs[13:16]
            self.yq, self.yp, self.full = refs[16:19]
            w = [e, 5 * e, 5 * e]
            self.width = w
            self.begin = [0, 4 * e, 9 * e]
            self.order = "zx", "zx", "xz"

        def pair(self, filters):
            filters(1 - core, self.out, BF)
            self.link = put(self.out, self.other, sib)

        def start(self):
            arrived([self.link])

            def body(n):
                at = pl.ds(pl.multiple_of(n * 16, 16), 16)
                total = self.own[at] + self.other[at].astype(F32)
                self.chip[lax.div(n, 4), lax.rem(n, 4)] = total.astype(BF)

            loop(16, body)
            e = self.e
            self.copies = []
            for o in (1, 2, 3):
                to = lax.rem(y + o, 4)
                at = pl.ds(pl.multiple_of(to * e, e), e)
                self.copies.append(put(self.chip.at[:, :, :, at], self.yr.at[o - 1], {"y": to}))
            self.first = [None, self.send_first(1), self.send_first(2)]

        def source(self, part):
            if part == 0:
                return self.ys, pl.ds(0, self.e)
            return self.chip, pl.ds(self.begin[part], self.width[part])

        def send_first(self, part):
            src, at = self.source(part)
            name, me = ("z", z) if self.order[part][0] == "z" else ("x", x)
            out = []
            for o in (1, 2, 3):
                to = lax.rem(me + o, 4)
                view = src.at[to, :, :, at] if name == "z" else src.at[:, to, :, at]
                out.append(put(view, self.recv[part][0].at[o - 1], {name: to}))
            return out

        def shared(self):
            arrived(self.copies)
            e = self.e
            at = pl.ds(pl.multiple_of(y * e, e), e)

            def body(n):
                total = self.chip[n, :, :, at].astype(F32)
                for o in range(3):
                    total += self.yr[o, n].astype(F32)
                self.ys[n] = total.astype(BF)

            loop(4, body)
            self.first[0] = self.send_first(0)

        def second(self, part):
            arrived(self.first[part])
            src, at = self.source(part)
            got, mid, _ = self.recv[part]
            total = (src[z, :, :, at] if self.order[part][0] == "z" else src[:, x, :, at]).astype(F32)
            for o in range(3):
                total += got[o].astype(F32)
            mid[...] = total.astype(BF)
            name, me = ("x", x) if self.order[part][0] == "z" else ("z", z)
            out = []
            for o in (1, 2, 3):
                to = lax.rem(me + o, 4)
                out.append(put(mid.at[to], self.recv[part][2].at[o - 1], {name: to}))
            self.first[part] = out

        def third(self, part):
            arrived(self.first[part])
            _, mid, got = self.recv[part]
            total = (mid[x] if self.order[part][0] == "z" else mid[z]).astype(F32)
            for o in range(3):
                total += got[o].astype(F32)
            e = self.e
            if part == 0:
                self.fin[y] = total.astype(BF)
                self.last0 = [put(self.fin.at[y], self.fin.at[y], along("y", y, o)) for o in (1, 2, 3)]
            else:
                at = slice((part - 1) * 5 * e, part * 5 * e)
                self.yq[:, at] = total.astype(BF)

        def fourth(self):
            self.last1 = [put(self.yq, self.yp.at[o - 1], along("y", y, o)) for o in (1, 2, 3)]

        def final(self):
            e = self.e
            arrived(self.last0)
            for n in range(4):
                self.full[core, :, n * e : (n + 1) * e] = self.fin[n].astype(F32)
            arrived(self.last1)
            total = self.yq[...].astype(F32)
            for o in range(3):
                total += self.yp[o].astype(F32)
            self.full[core, :, 4 * e : 14 * e] = total
            self.done = put(self.full.at[core], self.full.at[core], sib)

    sum1, sum2 = Sum(sums1, 128), Sum(sums2, 256)
    arrived(hid_halo)

    @pl.when(space == 0)
    def _():
        hid[:, 0] = jnp.zeros((2, 4, 32, 256), BF)

    def hidden_patches(v):
        for p in range(5):
            for q in range(2):
                fill = hid[q, p, v].astype(F32)
                parts = []
                for t in range(2):
                    fa[p, 8:40, :] = fill[:, t * 128 : (t + 1) * 128]
                    parts.append([fa[p, pl.ds(7 + k, 16, 2), :].astype(BF) for k in range(3)])
                for a, i in uses(p, 2):
                    for j in (1,) if q == 0 else (0, 2):
                        for k in range(3):
                            h, l = slot(9 * i + 3 * j + k)
                            for t in range(2):
                                im2[h, a, v, :, l * 256 + t * 128 : l * 256 + (t + 1) * 128] = parts[t][k]

    loop(4, hidden_patches)

    sum2.pair(second_filters)
    second_filters(core, sum2.own, F32)
    sum2.start()
    arrived(w2_last)

    cot_at = (cot0, cot1)
    for s1 in range(2):
        for s2 in range(2):
            for s3 in range(2):
                total = jnp.zeros((128, 256), F32)
                for i, d1 in PARITY[s1]:
                    for j, d2 in PARITY[s2]:
                        for k, d3 in PARITY[s3]:
                            h, l = slot(9 * i + 3 * j + k)
                            total += dot(
                                cot_at[d3][d2, d1 : d1 + 2].reshape(128, 256),
                                wf2[h, :, :, :, l * 256 : (l + 1) * 256].reshape(256, 256),
                            )
                for a in range(2):
                    for v in range(4):
                        n = (a * 4 + v) * 16
                        for t in range(2):
                            ab[s2, 2 * a + s1, v, t, pl.ds(s3, 16, 2), :] = total[n : n + 16, t * 128 : (t + 1) * 128]

    def back(q):
        for p in range(4):
            slope = jnp.where(pre[q, p] > 0, 1.0, 0.3)
            act_back = jnp.concatenate([ab[q, p, :, 0], ab[q, p, :, 1]], axis=-1)
            rows = act_back * slope
            pb0[q, p] = rows.astype(BF)
            pbt[q, p] = rows.reshape(128, 256).T.astype(BF)

    loop(2, back)
    pb_halo = [
        put(pb0.at[0, 0:4], pb0.at[2, 0:4], chan_at(15)),
        put(pb0.at[0:2, 0], pb0.at[0:2, 4], space_at(7)),
        put(pb0.at[0, 0], pb0.at[2, 4], {**space_at(7), **chan_at(15)}),
    ]

    sum1.pair(first_filters)
    first_filters(core, sum1.own, F32)
    sum1.start()

    for row in range(2):
        total = jnp.zeros((256, 128), F32)
        for tap in range(27):
            if (tap // 3 % 3 == 0) == (row == 1):
                h, l = slot(tap)
                at = slice(l * 256, (l + 1) * 256)
                total += dot_nt(wf2[h, :, :, :, at].reshape(256, 256), im2[h, :, :, :, at].reshape(128, 256))
        ot[:, row] = total.astype(BF).reshape(16, 16, 128)
    outs = []
    for o in range(1, 16):
        dev = chan_at(o)
        outs.append(put(ot.at[dev["z"] * 4 + dev["x"]], sor.at[chan], dev))
    sor[chan] = ot[chan]
    arrived(pb_halo[1:2])

    @pl.when(space == 7)
    def _():
        pb0[0:2, 4] = jnp.zeros((2, 4, 32, 256), BF)

    edge = lax.broadcasted_iota(jnp.int32, (128, 256), 0) % 32 == 31

    def shifted(q):
        for p in range(5):
            rows = pb0[q, p].reshape(128, 256).astype(F32)
            rows = jnp.where(edge, 0.0, pltpu.roll(rows, 127, 0))
            pb1[q, p] = rows.astype(BF).reshape(4, 32, 256)

    loop(2, shifted)

    def volume_grad(q):
        def body(n):
            for s1 in range(2):
                for s2 in range(2):
                    total = jnp.zeros((256, 256), F32)
                    extra = jnp.zeros((256, 128), F32)
                    for i, d1 in PARITY[s1]:
                        for j, d2 in PARITY[s2]:
                            h, l = slot(9 * i + 3 * j + 1)
                            total += dot(
                                pb0[q + d2, pl.ds(2 * n + d1, 2)].reshape(256, 256),
                                wf1[h, :, :, :, l * 128 : (l + 2) * 128].reshape(256, 256),
                            )
                            h, l = slot(9 * i + 3 * j)
                            extra += dot(
                                pb1[q + d2, pl.ds(2 * n + d1, 2)].reshape(256, 256),
                                wf1[h, :, :, :, l * 128 : (l + 1) * 128].reshape(256, 128),
                            )
                    extra += total[:, 128:]
                    for p in range(2):
                        for v in range(4):
                            m = (p * 4 + v) * 32
                            vs[p * 4 + v, pl.ds(0, 32, 2), :] = total[m : m + 32, 0:128]
                            vs[p * 4 + v, pl.ds(1, 32, 2), :] = extra[m : m + 32]
                            vg[v, 4 * n + 2 * p + s1, 2 * q + s2] = vs[p * 4 + v].astype(BF)

        loop(2, body)

    volume_grad(0)
    sum2.shared()
    sum2.second(1)
    sum2.second(2)
    sum1.shared()
    sum2.second(0)
    sum1.second(1)
    sum1.second(2)
    for part in (1, 2):
        sum2.third(part)
    sum2.fourth()
    sum1.second(0)
    sum2.third(0)
    arrived(pb_halo[0:1] + pb_halo[2:3])

    @pl.when(chan == 15)
    def _():
        pb0[2] = jnp.zeros((5, 4, 32, 256), BF)

    @pl.when(space == 7)
    def _():
        pb0[2, 4] = jnp.zeros((4, 32, 256), BF)

    shifted(2)
    for part in (1, 2):
        sum1.third(part)
    sum1.fourth()
    sum1.third(0)
    volume_grad(1)
    sum2.final()
    arrived(outs)
    so[0] = sor[0, 0]
    for b in range(1, 16):
        so[b] = (sor[b, 0].astype(F32) + sor[b - 1, 1].astype(F32)).astype(BF)
    sum1.final()
    arrived([sum2.done])
    for h in range(2):
        g2[h] = sum2.full[h]
    arrived([sum1.done])
    for h in range(2):
        g1[h] = sum1.full[h]
    for copy in sent:
        copy.wait_send()
    vol_half.copy.wait_send()


def finish(so, vg, g1, g2, so_out, vg_out, g1_out, g2_out, held, sem):
    loads = [pltpu.make_async_copy(vg.at[v], held.at[v], sem.at[0, v]) for v in range(4)]
    stores = [pltpu.make_async_copy(held.at[v], vg_out.at[v], sem.at[1, v]) for v in range(4)]
    for copy in loads:
        copy.start()
    for v in range(4):
        loads[v].wait()
        stores[v].start()
    rows = so[...].reshape(256, 128).astype(F32).T.astype(BF)
    for b in range(16):
        for a in range(2):
            for v in range(4):
                n = (a * 4 + v) * 16
                so_out[v, a, b] = rows[n : n + 16, 16 * b : 16 * b + 16]
    for tap in range(27):
        h, l = slot(tap)
        g1_out[tap] = g1[h, :, l * 128 : (l + 1) * 128]
        g2_out[tap] = g2[h, :, l * 256 : (l + 1) * 256]
    for copy in stores:
        copy.wait()


NSUM = 19


def sums(e):
    per_part = []
    for width, part in ((e, 0), (5 * e, 1), (5 * e, 2)):
        per_part += [
            pltpu.VMEM((3, 4, 16, width), BF),
            pltpu.VMEM((4, 16, width), BF),
            pltpu.VMEM((3, 16, width), BF),
        ]
    return [
        pltpu.VMEM((256, 14 * e), F32),
        pltpu.VMEM((256, 14 * e), BF),
        pltpu.VMEM((256, 14 * e), BF),
        pltpu.VMEM((4, 4, 16, 14 * e), BF),
        pltpu.VMEM((3, 4, 4, 16, e), BF),
        pltpu.VMEM((4, 4, 16, e), BF),
        pltpu.VMEM((4, 16, e), BF),
        *per_part,
        pltpu.VMEM((16, 10 * e), BF),
        pltpu.VMEM((3, 16, 10 * e), BF),
        pltpu.VMEM((2, 16, 14 * e), F32),
    ]


def local(volume, w_first, w_second, cotangent):
    w1 = jnp.swapaxes(w_first, 3, 4).reshape(27, 16, 128)
    w2 = jnp.swapaxes(w_second, 3, 4).reshape(27, 16, 256)
    vmem, anywhere = pl.BlockSpec(memory_space=pltpu.VMEM), pl.BlockSpec(memory_space=pl.ANY)
    so, vg, g1, g2 = pl.pallas_call(
        kernel,
        out_shape=(
            jax.ShapeDtypeStruct((16, 16, 128), BF),
            jax.ShapeDtypeStruct((4, 8, 4, 64, 128), BF),
            jax.ShapeDtypeStruct((2, 16, 1792), F32),
            jax.ShapeDtypeStruct((2, 16, 3584), F32),
        ),
        in_specs=[anywhere, vmem, vmem, anywhere],
        out_specs=(vmem, vmem, vmem, vmem),
        scratch_shapes=[
            pltpu.VMEM((4, 9, 5, 64, 128), BF),
            pltpu.VMEM((2, 2, 4, 4, 32, 1792), BF),
            pltpu.VMEM((2, 2, 4, 16, 3584), BF),
            pltpu.VMEM((2, 4, 4, 16, 1792), BF),
            pltpu.VMEM((2, 4, 4, 16, 3584), BF),
            pltpu.VMEM((2, 16, 1792), BF),
            pltpu.VMEM((2, 16, 3584), BF),
            pltpu.VMEM((2, 4, 4, 32, 256), F32),
            pltpu.VMEM((2, 4, 4, 2, 32, 128), F32),
            pltpu.VMEM((2, 5, 4, 32, 256), BF),
            pltpu.VMEM((3, 5, 4, 32, 256), BF),
            pltpu.VMEM((3, 5, 4, 32, 256), BF),
            pltpu.VMEM((2, 4, 256, 128), BF),
            pltpu.VMEM((4, 2, 16, 16, 16), BF),
            pltpu.VMEM((17, 16, 128), BF),
            pltpu.VMEM((2, 16, 16, 128), BF),
            pltpu.VMEM((2, 3, 4, 16, 256), BF),
            pltpu.VMEM((2, 3, 4, 16, 256), BF),
            pltpu.VMEM((5, 72, 128), F32),
            pltpu.VMEM((8, 64, 128), F32),
            *sums(128),
            *sums(256),
            pltpu.VMEM((16, 2, 16, 128), BF),
            pltpu.VMEM((16, 2, 16, 128), BF),
            pltpu.VMEM((2, 8, 64, 128), BF),
            pltpu.SemaphoreType.DMA((NSEM,)),
            pltpu.SemaphoreType.DMA((NSEM,)),
            pltpu.SemaphoreType.DMA((2,)),
            pltpu.SemaphoreType.DMA((2,)),
            pltpu.SemaphoreType.DMA((2,)),
        ],
        compiler_params=pltpu.CompilerParams(
            collective_id=0, has_side_effects=True, vmem_limit_bytes=56 * 1024 * 1024
        ),
        cost_estimate=pl.CostEstimate(flops=6_800_000_000, bytes_accessed=6_000_000, transcendentals=0),
        name="two_layers",
    )(volume, w1, w2, cotangent)
    so, vg, g1, g2 = pl.pallas_call(
        finish,
        out_shape=(
            jax.ShapeDtypeStruct((4, 2, 16, 16, 16), BF),
            jax.ShapeDtypeStruct((4, 8, 4, 64, 128), BF),
            jax.ShapeDtypeStruct((27, 16, 128), F32),
            jax.ShapeDtypeStruct((27, 16, 256), F32),
        ),
        in_specs=[vmem, anywhere, vmem, vmem],
        out_specs=(vmem, anywhere, vmem, vmem),
        scratch_shapes=[pltpu.VMEM((4, 8, 4, 64, 128), BF), pltpu.SemaphoreType.DMA((2, 4))],
        name="finish",
    )(so, vg, g1, g2)
    g1 = jnp.swapaxes(g1.reshape(3, 3, 3, 16, 128), 3, 4)
    g2 = jnp.swapaxes(g2.reshape(3, 3, 3, 16, 256), 3, 4)
    return so, vg, g1, g2


def solution(mesh):
    space, chan = ("y", "core"), ("z", "x")
    finer = Mesh(mesh.devices.reshape(4, 2, 4, 4), (*space, *chan))
    return jax.shard_map(
        local,
        mesh=finer,
        in_specs=(
            P(None, space, chan, None, None),
            P(None, None, None, None, chan),
            P(None, None, None, None, chan),
            P(None, space, None, None, chan),
        ),
        out_specs=(
            P(None, space, None, None, chan),
            P(None, space, chan, None, None),
            P(None, None, None, None, chan),
            P(None, None, None, None, chan),
        ),
        check_vma=False,
    )
```

```python
import jax
import jax.numpy as jnp
from jax import lax
from jax.experimental import pallas as pl
from jax.experimental.pallas import tpu as pltpu
from jax.sharding import Mesh
from jax.sharding import PartitionSpec as P

MESH = pl.DeviceIdType.MESH
BF = jnp.bfloat16
F32 = jnp.float32
NSEM = 160

SLOT = {}
for _g in range(9):
    _base = 2 * _g if _g < 5 else 14 + 2 * (_g - 5)
    SLOT[3 * _g + 1], SLOT[3 * _g + 2] = _base, _base + 1
    SLOT[3 * _g] = 10 + _g if _g < 4 else 22 + (_g - 4)


def slot(tap):
    return divmod(SLOT[tap], 14)


def uses(cell, count):
    return [(o, cell - 2 * o) for o in range(count) if 0 <= cell - 2 * o <= 2]


PARITY = (((1, 0),), ((0, 1), (2, 0)))


def dot(a, b):
    return lax.dot_general(a, b, (((1,), (0,)), ((), ())), preferred_element_type=F32)


def dot_nt(a, b):
    return lax.dot_general(a, b, (((1,), (1,)), ((), ())), preferred_element_type=F32)


def loop(count, body):
    def step(i, carry):
        body(i)
        return carry

    lax.fori_loop(0, count, step, 0)


def kernel(
    vol, w1, w2, cot, so, vg, g1, g2,
    xv, im1, im2, wf1, wf2, w1o, w2o, pre, ab, hid, pb0, pb1, pbt, cotv, cotl, cott, cot0, cot1, fa, vs,
    *rest,
):
    sums1, sums2 = rest[:NSUM], rest[NSUM : 2 * NSUM]
    ot, sor, vgv, relay, ssem, rsem, lsem, hsend, hrecv = rest[2 * NSUM :]
    y, core = lax.axis_index("y"), lax.axis_index("core")
    z, x = lax.axis_index("z"), lax.axis_index("x")
    chan = z * 4 + x
    space = y * 2 + core
    sib = {"core": 1 - core}

    def along(name, me, off):
        return {name: lax.rem(me + off, 4)}

    def chan_at(off):
        c = lax.rem(chan + off, 16)
        return {"z": lax.div(c, 4), "x": lax.rem(c, 4)}

    def space_at(off):
        s = lax.rem(space + off, 8)
        return {"y": lax.div(s, 2), "core": lax.rem(s, 2)}

    sent = []

    def put(src, dst, dev):
        n = len(sent)
        copy = pltpu.make_async_remote_copy(
            src_ref=src, dst_ref=dst, send_sem=ssem.at[n], recv_sem=rsem.at[n],
            device_id=dev, device_id_type=MESH,
        )
        copy.start()
        sent.append(copy)
        return copy

    class hold:
        def __init__(self, src, dst, dev):
            n = count[0]
            count[0] += 1
            self.send, self.recv = hsend.at[n], hrecv.at[n]
            self.copy = pltpu.make_async_remote_copy(
                src_ref=src, dst_ref=dst, send_sem=self.send, recv_sem=self.recv,
                device_id=dev, device_id_type=MESH,
            )

    count = [0]

    def arrived(copies):
        for copy in copies:
            copy.wait_recv()

    cells = pltpu.make_async_copy(cot, cotv, lsem.at[1])
    cells.start()
    local = pltpu.make_async_copy(vol, xv.at[:, 1:9, 1:5], lsem.at[0])
    local.start()

    barrier = pltpu.get_barrier_semaphore()
    partners = [chan_at(o) for o in range(1, 16)]
    partners += [along("y", y, o) for o in range(1, 4)]
    partners += [sib, {"y": lax.rem(y + 3 + 2 * core, 4), "core": 1 - core}]
    partners += [{**space_at(1), **chan_at(1)}, {**space_at(7), **chan_at(15)}]
    for dev in partners:
        pl.semaphore_signal(barrier, inc=1, device_id=dev, device_id_type=MESH)

    for tap in range(27):
        h, l = slot(tap)
        w1o[h, :, l * 128 : (l + 1) * 128] = w1[tap]
        w2o[h, :, l * 256 : (l + 1) * 256] = w2[tap]
    w1o[1, :, 13 * 128 :] = jnp.zeros((16, 128), BF)
    w2o[1, :, 13 * 256 :] = jnp.zeros((16, 256), BF)
    for own, full, q, rest_at in ((w1o, wf1, 128, 512), (w2o, wf2, 256, 1024)):
        at = pl.ds(pl.multiple_of(y * q, q), q)
        full[core, z, x, :, at] = own[core, :, at]
        full[core, z, x, :, rest_at:] = own[core, :, rest_at:]

    pl.semaphore_wait(barrier, len(partners))

    def cut(e, shared, direct):
        q = shared // 4 * e
        return (
            pl.ds(pl.multiple_of(y * q, q), q),
            pl.ds(shared * e, direct * e),
            pl.ds((shared + direct) * e, (14 - shared - direct) * e),
        )

    def one_row(own, full, at, name):
        me = x if name == "x" else z
        return [put(own.at[core, :, at], full.at[core, z, x, :, at], along(name, me, o)) for o in (1, 2, 3)]

    def four_rows(full, at, name, before):
        arrived(before)
        part = full.at[core, z, :, :, at] if name == "z" else full.at[core, :, x, :, at]
        return [put(part, part, along(name, x if name == "x" else z, o)) for o in (1, 2, 3)]

    def all_rows(full, at, before):
        arrived(before)
        part = full.at[core, :, :, :, at]
        return [put(part, part, along("y", y, o)) for o in (1, 2, 3)]

    def spread_last(full, at, copies):
        arrived(copies)
        part = full.at[core, :, :, :, at]
        return put(part, part, sib)

    (p1, q1, r1), (p2, q2, r2) = cut(128, 4, 5), cut(256, 4, 5)
    w1_px, w1_qx, w1_rz = one_row(w1o, wf1, p1, "x"), one_row(w1o, wf1, q1, "x"), one_row(w1o, wf1, r1, "z")
    w2_px, w2_rz, w2_qx = one_row(w2o, wf2, p2, "x"), one_row(w2o, wf2, r2, "z"), one_row(w2o, wf2, q2, "x")
    vol_plane = put(vol.at[:, 7], xv.at[:, 0, 1:5], space_at(1))

    cells.wait()
    unit = (lax.broadcasted_iota(jnp.int32, (16, 16), 0) == lax.broadcasted_iota(jnp.int32, (16, 16), 1)).astype(BF)
    for b in range(16):
        row = jnp.concatenate([cotv[v, a, b] for a in range(2) for v in range(4)], axis=0)
        cotl[b] = dot_nt(unit, row).astype(BF)
    cotl[16] = jnp.zeros((16, 128), BF)
    cots = []
    for o in range(1, 16):
        dev = chan_at(o)
        row = dev["z"] * 4 + dev["x"]
        cots.append(put(cotl.at[pl.ds(row, 2)], cott.at[:, chan], dev))
    cott[:, chan] = cotl[pl.ds(chan, 2)]

    w1_pz = four_rows(wf1, p1, "z", w1_px)
    w2_pz = four_rows(wf2, p2, "z", w2_px)
    w1_rx = four_rows(wf1, r1, "x", w1_rz)
    w1_qz = four_rows(wf1, q1, "z", w1_qx)

    vol_row = [
        put(vol.at[0:2, :, 3], xv.at[0:2, 1:9, 0], chan_at(1)),
        put(vol.at[:, 7, 3], xv.at[:, 0, 0], {**space_at(1), **chan_at(1)}),
    ]
    vol_step, vol_half = hold(vol.at[2:4, :, 3], relay, {"z": lax.rem(z + 1, 4)}), hold(vol.at[2:4, :, 3], xv.at[2:4, 1:9, 0], chan_at(1))
    vol_on = pltpu.make_async_remote_copy(
        src_ref=relay, dst_ref=xv.at[2:4, 1:9, 0], send_sem=vol_half.send, recv_sem=vol_half.recv,
        device_id=along("x", x, 1), device_id_type=MESH,
    )

    @pl.when(x == 3)
    def _():
        vol_step.copy.start()

    @pl.when(x != 3)
    def _():
        vol_half.copy.start()

    w2_rx = four_rows(wf2, r2, "x", w2_rz)
    w2_qz = four_rows(wf2, q2, "z", w2_qx)

    fa[:, 0:8, :] = jnp.zeros((5, 8, 128), F32)

    def patches(blocks):
        def body(v):
            for a, b in blocks:
                fa[b, 8:72, :] = xv[v, a, b].astype(F32)
                parts = [fa[b, pl.ds(7 + k, 32, 2), :].astype(BF) for k in range(3)]
                for p, i in uses(a, 4):
                    for q, j in uses(b, 2):
                        for k in range(3):
                            h, l = slot(9 * i + 3 * j + k)
                            im1[h, q, p, v, :, l * 128 : (l + 1) * 128] = parts[k]

        loop(4, body)

    def blank(v):
        for q in range(2):
            for p in range(4):
                im1[1, q, p, v, :, 13 * 128 :] = jnp.zeros((32, 128), BF)

    loop(4, blank)
    im2[1, :, :, :, 13 * 256 :] = jnp.zeros((2, 4, 16, 256), BF)
    local.wait()
    patches([(a, b) for a in range(1, 9) for b in range(1, 5)])
    w1_py = all_rows(wf1, p1, w1_pz)
    w2_py = all_rows(wf2, p2, w2_pz)
    @pl.when(x == 3)
    def _():
        vol_step.copy.wait()
        vol_on.start()

    arrived(cots)
    for b in range(2):
        rows = cott[b].reshape(256, 128).astype(F32).T.astype(BF)
        cot0[b, 0:2] = rows.reshape(2, 4, 16, 256)
    cot_halo = put(cot0.at[:, 0], cot0.at[:, 2], space_at(7))

    arrived([vol_plane])

    @pl.when(space == 0)
    def _():
        xv[:, 0, 1:5] = jnp.zeros((4, 4, 64, 128), BF)

    patches([(0, b) for b in range(1, 5)])

    w1_last = [
        spread_last(wf1, pl.ds(0, 512), w1_py),
        spread_last(wf1, pl.ds(512, 1280), w1_qz + w1_rx),
    ]
    arrived(w1_last)

    def conv_first(q):
        def body(n):
            total = jnp.zeros((256, 256), F32)
            for h in range(2):
                total += dot_nt(im1[h, q, pl.ds(2 * n, 2)].reshape(256, 1792), wf1[h].reshape(256, 1792))
            pre[q, pl.ds(2 * n, 2)] = total.reshape(2, 4, 32, 256)
            act = jnp.where(total > 0, total, 0.3 * total).astype(BF)
            hid[q, pl.ds(2 * n + 1, 2)] = act.reshape(2, 4, 32, 256)

        loop(2, body)

    conv_first(1)

    arrived([cot_halo])

    @pl.when(space == 7)
    def _():
        cot0[:, 2] = jnp.zeros((2, 4, 16, 256), BF)

    last = lax.broadcasted_iota(jnp.int32, (64, 256), 0) % 16 == 15
    for b in range(2):
        for a in range(3):
            rows = cot0[b, a].reshape(64, 256).astype(F32)
            rows = jnp.where(last, 0.0, pltpu.roll(rows, 63, 0))
            cot1[b, a] = rows.astype(BF).reshape(4, 16, 256)

    arrived(vol_row)
    vol_half.copy.wait_recv()

    @pl.when(chan == 0)
    def _():
        xv[:, :, 0] = jnp.zeros((4, 9, 64, 128), BF)

    @pl.when(space == 0)
    def _():
        xv[:, 0, 0] = jnp.zeros((4, 64, 128), BF)

    patches([(a, 0) for a in range(9)])
    conv_first(0)
    hid_halo = [put(hid.at[0:2, 4], hid.at[0:2, 0], space_at(1))]
    w2_last = [spread_last(wf2, pl.ds(0, 1024), w2_py), spread_last(wf2, pl.ds(1024, 2560), w2_qz + w2_rx)]

    def second_filters(half, dst, kind):
        def body(n):
            at = pl.ds(pl.multiple_of(n * 256, 256), 256)
            place = half * 14 + n
            following = jnp.int32(0)
            for tap in range(27):
                if tap // 3 % 3 == 0:
                    following += jnp.where(place == SLOT[tap], 1, 0)
            lhs = cott[following].reshape(256, 128)
            dst[:, at] = dot(lhs, im2[half, :, :, :, at].reshape(128, 256)).astype(kind)

        loop(14, body)

    def first_filters(half, dst, kind):
        lhs = jnp.concatenate([pbt[q, p] for q in range(2) for p in range(4)], axis=1)

        def body(n):
            at = pl.ds(pl.multiple_of(n * 256, 256), 256)
            dst[:, at] = dot(lhs, im1[half, :, :, :, :, at].reshape(1024, 256)).astype(kind)

        loop(7, body)

    class Sum:
        def __init__(self, refs, e):
            self.e = e
            (self.own, self.out, self.other, self.chip, self.yr, self.ys, self.fin) = refs[:7]
            self.recv = refs[7:10], refs[10:13], refs[13:16]
            self.yq, self.yp, self.full = refs[16:19]
            w = [e, 5 * e, 5 * e]
            self.width = w
            self.begin = [0, 4 * e, 9 * e]
            self.order = "zx", "zx", "xz"

        def pair(self, filters):
            filters(1 - core, self.out, BF)
            self.link = put(self.out, self.other, sib)

        def start(self):
            arrived([self.link])

            def body(n):
                at = pl.ds(pl.multiple_of(n * 16, 16), 16)
                total = self.own[at] + self.other[at].astype(F32)
                self.chip[lax.div(n, 4), lax.rem(n, 4)] = total.astype(BF)

            loop(16, body)
            e = self.e
            self.copies = []
            for o in (1, 2, 3):
                to = lax.rem(y + o, 4)
                at = pl.ds(pl.multiple_of(to * e, e), e)
                self.copies.append(put(self.chip.at[:, :, :, at], self.yr.at[o - 1], {"y": to}))
            self.first = [None, self.send_first(1), self.send_first(2)]

        def source(self, part):
            if part == 0:
                return self.ys, pl.ds(0, self.e)
            return self.chip, pl.ds(self.begin[part], self.width[part])

        def send_first(self, part):
            src, at = self.source(part)
            name, me = ("z", z) if self.order[part][0] == "z" else ("x", x)
            out = []
            for o in (1, 2, 3):
                to = lax.rem(me + o, 4)
                view = src.at[to, :, :, at] if name == "z" else src.at[:, to, :, at]
                out.append(put(view, self.recv[part][0].at[o - 1], {name: to}))
            return out

        def shared(self):
            arrived(self.copies)
            e = self.e
            at = pl.ds(pl.multiple_of(y * e, e), e)

            def body(n):
                total = self.chip[n, :, :, at].astype(F32)
                for o in range(3):
                    total += self.yr[o, n].astype(F32)
                self.ys[n] = total.astype(BF)

            loop(4, body)
            self.first[0] = self.send_first(0)

        def second(self, part):
            arrived(self.first[part])
            src, at = self.source(part)
            got, mid, _ = self.recv[part]
            total = (src[z, :, :, at] if self.order[part][0] == "z" else src[:, x, :, at]).astype(F32)
            for o in range(3):
                total += got[o].astype(F32)
            mid[...] = total.astype(BF)
            name, me = ("x", x) if self.order[part][0] == "z" else ("z", z)
            out = []
            for o in (1, 2, 3):
                to = lax.rem(me + o, 4)
                out.append(put(mid.at[to], self.recv[part][2].at[o - 1], {name: to}))
            self.first[part] = out

        def third(self, part):
            arrived(self.first[part])
            _, mid, got = self.recv[part]
            total = (mid[x] if self.order[part][0] == "z" else mid[z]).astype(F32)
            for o in range(3):
                total += got[o].astype(F32)
            e = self.e
            if part == 0:
                self.fin[y] = total.astype(BF)
                self.last0 = [put(self.fin.at[y], self.fin.at[y], along("y", y, o)) for o in (1, 2, 3)]
            else:
                at = slice((part - 1) * 5 * e, part * 5 * e)
                self.yq[:, at] = total.astype(BF)

        def fourth(self):
            self.last1 = [put(self.yq, self.yp.at[o - 1], along("y", y, o)) for o in (1, 2, 3)]

        def final(self):
            e = self.e
            arrived(self.last0)
            for n in range(4):
                self.full[core, :, n * e : (n + 1) * e] = self.fin[n].astype(F32)
            arrived(self.last1)
            total = self.yq[...].astype(F32)
            for o in range(3):
                total += self.yp[o].astype(F32)
            self.full[core, :, 4 * e : 14 * e] = total
            self.done = put(self.full.at[core], self.full.at[core], sib)

    sum1, sum2 = Sum(sums1, 128), Sum(sums2, 256)
    arrived(hid_halo)

    @pl.when(space == 0)
    def _():
        hid[:, 0] = jnp.zeros((2, 4, 32, 256), BF)

    def hidden_patches(v):
        for p in range(5):
            for q in range(2):
                fill = hid[q, p, v].astype(F32)
                parts = []
                for t in range(2):
                    fa[p, 8:40, :] = fill[:, t * 128 : (t + 1) * 128]
                    parts.append([fa[p, pl.ds(7 + k, 16, 2), :].astype(BF) for k in range(3)])
                for a, i in uses(p, 2):
                    for j in (1,) if q == 0 else (0, 2):
                        for k in range(3):
                            h, l = slot(9 * i + 3 * j + k)
                            for t in range(2):
                                im2[h, a, v, :, l * 256 + t * 128 : l * 256 + (t + 1) * 128] = parts[t][k]

    loop(4, hidden_patches)

    sum2.pair(second_filters)
    second_filters(core, sum2.own, F32)
    sum2.start()
    arrived(w2_last)

    cot_at = (cot0, cot1)
    for s1 in range(2):
        for s2 in range(2):
            for s3 in range(2):
                total = jnp.zeros((128, 256), F32)
                for i, d1 in PARITY[s1]:
                    for j, d2 in PARITY[s2]:
                        for k, d3 in PARITY[s3]:
                            h, l = slot(9 * i + 3 * j + k)
                            total += dot(
                                cot_at[d3][d2, d1 : d1 + 2].reshape(128, 256),
                                wf2[h, :, :, :, l * 256 : (l + 1) * 256].reshape(256, 256),
                            )
                for a in range(2):
                    for v in range(4):
                        n = (a * 4 + v) * 16
                        for t in range(2):
                            ab[s2, 2 * a + s1, v, t, pl.ds(s3, 16, 2), :] = total[n : n + 16, t * 128 : (t + 1) * 128]

    def back(q):
        for p in range(4):
            slope = jnp.where(pre[q, p] > 0, 1.0, 0.3)
            act_back = jnp.concatenate([ab[q, p, :, 0], ab[q, p, :, 1]], axis=-1)
            rows = act_back * slope
            pb0[q, p] = rows.astype(BF)
            pbt[q, p] = rows.reshape(128, 256).T.astype(BF)

    loop(2, back)
    pb_halo = [
        put(pb0.at[0, 0:4], pb0.at[2, 0:4], chan_at(15)),
        put(pb0.at[0:2, 0], pb0.at[0:2, 4], space_at(7)),
        put(pb0.at[0, 0], pb0.at[2, 4], {**space_at(7), **chan_at(15)}),
    ]

    sum1.pair(first_filters)
    first_filters(core, sum1.own, F32)
    sum1.start()

    for row in range(2):
        total = jnp.zeros((256, 128), F32)
        for tap in range(27):
            if (tap // 3 % 3 == 0) == (row == 1):
                h, l = slot(tap)
                at = slice(l * 256, (l + 1) * 256)
                total += dot_nt(wf2[h, :, :, :, at].reshape(256, 256), im2[h, :, :, :, at].reshape(128, 256))
        ot[:, row] = total.astype(BF).reshape(16, 16, 128)
    outs = []
    for o in range(1, 16):
        dev = chan_at(o)
        outs.append(put(ot.at[dev["z"] * 4 + dev["x"]], sor.at[chan], dev))
    sor[chan] = ot[chan]
    arrived(pb_halo[1:2])

    @pl.when(space == 7)
    def _():
        pb0[0:2, 4] = jnp.zeros((2, 4, 32, 256), BF)

    edge = lax.broadcasted_iota(jnp.int32, (128, 256), 0) % 32 == 31

    def shifted(q):
        for p in range(5):
            rows = pb0[q, p].reshape(128, 256).astype(F32)
            rows = jnp.where(edge, 0.0, pltpu.roll(rows, 127, 0))
            pb1[q, p] = rows.astype(BF).reshape(4, 32, 256)

    loop(2, shifted)

    def volume_grad(q):
        def body(n):
            for s1 in range(2):
                for s2 in range(2):
                    total = jnp.zeros((256, 256), F32)
                    extra = jnp.zeros((256, 128), F32)
                    for i, d1 in PARITY[s1]:
                        for j, d2 in PARITY[s2]:
                            h, l = slot(9 * i + 3 * j + 1)
                            total += dot(
                                pb0[q + d2, pl.ds(2 * n + d1, 2)].reshape(256, 256),
                                wf1[h, :, :, :, l * 128 : (l + 2) * 128].reshape(256, 256),
                            )
                            h, l = slot(9 * i + 3 * j)
                            extra += dot(
                                pb1[q + d2, pl.ds(2 * n + d1, 2)].reshape(256, 256),
                                wf1[h, :, :, :, l * 128 : (l + 1) * 128].reshape(256, 128),
                            )
                    extra += total[:, 128:]
                    for p in range(2):
                        for v in range(4):
                            m = (p * 4 + v) * 32
                            vs[p * 4 + v, pl.ds(0, 32, 2), :] = total[m : m + 32, 0:128]
                            vs[p * 4 + v, pl.ds(1, 32, 2), :] = extra[m : m + 32]
                            vgv[v, 4 * n + 2 * p + s1, 2 * q + s2] = vs[p * 4 + v].astype(BF)

        loop(2, body)

    volume_grad(0)
    grads = [pltpu.make_async_copy(vgv.at[:, :, 0:2], vg.at[:, :, 0:2], lsem.at[0])]
    grads[0].start()
    sum2.shared()
    sum2.second(1)
    sum2.second(2)
    sum1.shared()
    sum2.second(0)
    sum1.second(1)
    sum1.second(2)
    for part in (1, 2):
        sum2.third(part)
    sum2.fourth()
    sum1.second(0)
    sum2.third(0)
    arrived(pb_halo[0:1] + pb_halo[2:3])

    @pl.when(chan == 15)
    def _():
        pb0[2] = jnp.zeros((5, 4, 32, 256), BF)

    @pl.when(space == 7)
    def _():
        pb0[2, 4] = jnp.zeros((4, 32, 256), BF)

    shifted(2)
    for part in (1, 2):
        sum1.third(part)
    sum1.fourth()
    sum1.third(0)
    volume_grad(1)
    grads.append(pltpu.make_async_copy(vgv.at[:, :, 2:4], vg.at[:, :, 2:4], lsem.at[1]))
    grads[1].start()
    sum2.final()
    arrived(outs)
    so[0] = sor[0, 0]
    for b in range(1, 16):
        so[b] = (sor[b, 0].astype(F32) + sor[b - 1, 1].astype(F32)).astype(BF)
    sum1.final()
    arrived([sum2.done])
    for h in range(2):
        g2[h] = sum2.full[h]
    arrived([sum1.done])
    for h in range(2):
        g1[h] = sum1.full[h]
    for copy in grads:
        copy.wait()
    for copy in sent:
        copy.wait_send()
    vol_half.copy.wait_send()


def finish(so, vg, g1, g2, so_out, vg_out, g1_out, g2_out, held, sem):
    loads = [pltpu.make_async_copy(vg.at[v], held.at[v], sem.at[0, v]) for v in range(4)]
    stores = [pltpu.make_async_copy(held.at[v], vg_out.at[v], sem.at[1, v]) for v in range(4)]
    for copy in loads:
        copy.start()
    for v in range(4):
        loads[v].wait()
        stores[v].start()
    rows = so[...].reshape(256, 128).astype(F32).T.astype(BF)
    for b in range(16):
        for a in range(2):
            for v in range(4):
                n = (a * 4 + v) * 16
                so_out[v, a, b] = rows[n : n + 16, 16 * b : 16 * b + 16]
    for tap in range(27):
        h, l = slot(tap)
        g1_out[tap] = g1[h, :, l * 128 : (l + 1) * 128]
        g2_out[tap] = g2[h, :, l * 256 : (l + 1) * 256]
    for copy in stores:
        copy.wait()


NSUM = 19


def sums(e):
    per_part = []
    for width, part in ((e, 0), (5 * e, 1), (5 * e, 2)):
        per_part += [
            pltpu.VMEM((3, 4, 16, width), BF),
            pltpu.VMEM((4, 16, width), BF),
            pltpu.VMEM((3, 16, width), BF),
        ]
    return [
        pltpu.VMEM((256, 14 * e), F32),
        pltpu.VMEM((256, 14 * e), BF),
        pltpu.VMEM((256, 14 * e), BF),
        pltpu.VMEM((4, 4, 16, 14 * e), BF),
        pltpu.VMEM((3, 4, 4, 16, e), BF),
        pltpu.VMEM((4, 4, 16, e), BF),
        pltpu.VMEM((4, 16, e), BF),
        *per_part,
        pltpu.VMEM((16, 10 * e), BF),
        pltpu.VMEM((3, 16, 10 * e), BF),
        pltpu.VMEM((2, 16, 14 * e), F32),
    ]


def local(volume, w_first, w_second, cotangent):
    w1 = jnp.swapaxes(w_first, 3, 4).reshape(27, 16, 128)
    w2 = jnp.swapaxes(w_second, 3, 4).reshape(27, 16, 256)
    vmem, anywhere = pl.BlockSpec(memory_space=pltpu.VMEM), pl.BlockSpec(memory_space=pl.ANY)
    so, vg, g1, g2 = pl.pallas_call(
        kernel,
        out_shape=(
            jax.ShapeDtypeStruct((16, 16, 128), BF),
            jax.ShapeDtypeStruct((4, 8, 4, 64, 128), BF),
            jax.ShapeDtypeStruct((2, 16, 1792), F32),
            jax.ShapeDtypeStruct((2, 16, 3584), F32),
        ),
        in_specs=[anywhere, vmem, vmem, anywhere],
        out_specs=(vmem, anywhere, vmem, vmem),
        scratch_shapes=[
            pltpu.VMEM((4, 9, 5, 64, 128), BF),
            pltpu.VMEM((2, 2, 4, 4, 32, 1792), BF),
            pltpu.VMEM((2, 2, 4, 16, 3584), BF),
            pltpu.VMEM((2, 4, 4, 16, 1792), BF),
            pltpu.VMEM((2, 4, 4, 16, 3584), BF),
            pltpu.VMEM((2, 16, 1792), BF),
            pltpu.VMEM((2, 16, 3584), BF),
            pltpu.VMEM((2, 4, 4, 32, 256), F32),
            pltpu.VMEM((2, 4, 4, 2, 32, 128), F32),
            pltpu.VMEM((2, 5, 4, 32, 256), BF),
            pltpu.VMEM((3, 5, 4, 32, 256), BF),
            pltpu.VMEM((3, 5, 4, 32, 256), BF),
            pltpu.VMEM((2, 4, 256, 128), BF),
            pltpu.VMEM((4, 2, 16, 16, 16), BF),
            pltpu.VMEM((17, 16, 128), BF),
            pltpu.VMEM((2, 16, 16, 128), BF),
            pltpu.VMEM((2, 3, 4, 16, 256), BF),
            pltpu.VMEM((2, 3, 4, 16, 256), BF),
            pltpu.VMEM((5, 72, 128), F32),
            pltpu.VMEM((8, 64, 128), F32),
            *sums(128),
            *sums(256),
            pltpu.VMEM((16, 2, 16, 128), BF),
            pltpu.VMEM((16, 2, 16, 128), BF),
            pltpu.VMEM((4, 8, 4, 64, 128), BF),
            pltpu.VMEM((2, 8, 64, 128), BF),
            pltpu.SemaphoreType.DMA((NSEM,)),
            pltpu.SemaphoreType.DMA((NSEM,)),
            pltpu.SemaphoreType.DMA((2,)),
            pltpu.SemaphoreType.DMA((2,)),
            pltpu.SemaphoreType.DMA((2,)),
        ],
        compiler_params=pltpu.CompilerParams(
            collective_id=0, has_side_effects=True, vmem_limit_bytes=56 * 1024 * 1024
        ),
        cost_estimate=pl.CostEstimate(flops=6_800_000_000, bytes_accessed=6_000_000, transcendentals=0),
        name="two_layers",
    )(volume, w1, w2, cotangent)
    so, vg, g1, g2 = pl.pallas_call(
        finish,
        out_shape=(
            jax.ShapeDtypeStruct((4, 2, 16, 16, 16), BF),
            jax.ShapeDtypeStruct((4, 8, 4, 64, 128), BF),
            jax.ShapeDtypeStruct((27, 16, 128), F32),
            jax.ShapeDtypeStruct((27, 16, 256), F32),
        ),
        in_specs=[vmem, anywhere, vmem, vmem],
        out_specs=(vmem, anywhere, vmem, vmem),
        scratch_shapes=[pltpu.VMEM((4, 8, 4, 64, 128), BF), pltpu.SemaphoreType.DMA((2, 4))],
        name="finish",
    )(so, vg, g1, g2)
    g1 = jnp.swapaxes(g1.reshape(3, 3, 3, 16, 128), 3, 4)
    g2 = jnp.swapaxes(g2.reshape(3, 3, 3, 16, 256), 3, 4)
    return so, vg, g1, g2


def solution(mesh):
    space, chan = ("y", "core"), ("z", "x")
    finer = Mesh(mesh.devices.reshape(4, 2, 4, 4), (*space, *chan))
    return jax.shard_map(
        local,
        mesh=finer,
        in_specs=(
            P(None, space, chan, None, None),
            P(None, None, None, None, chan),
            P(None, None, None, None, chan),
            P(None, space, None, None, chan),
        ),
        out_specs=(
            P(None, space, None, None, chan),
            P(None, space, chan, None, None),
            P(None, None, None, None, chan),
            P(None, None, None, None, chan),
        ),
        check_vma=False,
    )
```
